32 devices in a mesh: gx: 8 (over y, x, core), ch: 4 (over z).
Axes of the slice: x: 2, y: 2, z: 4, core: 2. Of those that a mesh axis runs over, the one named last changes fastest.
Arguments:
- activations: bfloat16 [128, 128, 4, 128], P('ch', 'gx'), may hold values from -6 to 6
- conv_weight: bfloat16 [27, 128, 128], P(None, None, 'ch'), may hold values from -0.109375 to 0.109375
- out_grad: bfloat16 [128, 128, 4, 128], P('ch', 'gx'), may hold values from -6 to 6
Outputs:
- features_out: bfloat16 [128, 128, 4, 128], P('ch', 'gx')
- input_grad: bfloat16 [128, 128, 4, 128], P('ch', 'gx')
The draws below stay inside these ranges and needn't reach their ends.
All inputs are finite; a program needn't handle non-finite values.
Results may differ from the reference program's by a relative error of at most 0.001.
Values may be sent and summed in bfloat16 or wider, within the bound.
A program may use at most 64 MiB of HBM per device.

```python
import jax
import jax.numpy as jnp

C = 128
YW = 128
ZW = 4
X = 128


def levels(key, shape, split, least, high):
    gain, own = 1.0, jax.random.fold_in(key, 6)
    for axis_at, parts in split:
        draws = jnp.exp(jax.random.uniform(jax.random.fold_in(own, axis_at), (parts,), jnp.float32, least / len(split), high / len(split)))
        gain = gain * jnp.repeat(draws, shape[axis_at] // parts).reshape([-1 if axis == axis_at else 1 for axis in range(len(shape))])
    return gain


def gaussian(own_key, dims, width, bound, pieces=(), dtype=jnp.bfloat16):
    result = jax.random.normal(own_key, dims, jnp.float32) * width
    if len(pieces) > 0:
        result = levels(own_key, dims, pieces, -0.22, 0.18) * result
    return jnp.clip(result, min=-bound, max=bound).astype(dtype)


def setup_inputs(seed: int = 0) -> dict:
    streams_of = jax.random.split(jax.random.key(seed), 4)
    return {
        "activations": gaussian(streams_of[0], (C, X, ZW, YW), 1.0, 6.0, ((0, 4), (1, 8))),
        "conv_weight": gaussian(streams_of[1], (27, C, C), (27 * C) ** -0.5, 0.109375, ((2, 4),)),
        "out_grad": gaussian(streams_of[2], (C, X, ZW, YW), 1.0, 6.0, ((0, 4), (1, 8))),
    }


def shifted(field, along_x, along_y, along_z):
    rolled = jnp.roll(field, -along_x, axis=1)
    padded = jnp.pad(rolled, ((0, 0), (0, 0), (1, 1), (1, 1)))
    return padded[:, :, 1 + along_z:1 + along_z + ZW, 1 + along_y:1 + along_y + YW]


def reference(activations, conv_weight, out_grad):
    summed_out = jnp.zeros((C, X * ZW * YW), jnp.float32)
    summed_grad = jnp.zeros((C, X * ZW * YW), jnp.float32)
    for first in range(3):
        for second in range(3):
            for third in range(3):
                tap = 9 * first + 3 * second + third
                source = shifted(activations, first - 1, second - 1, third - 1).reshape(C, -1)
                summed_out = summed_out + jnp.dot(conv_weight[tap].T, source, preferred_element_type=jnp.float32)
                back = shifted(out_grad, 1 - first, 1 - second, 1 - third).reshape(C, -1)
                summed_grad = summed_grad + jnp.dot(conv_weight[tap], back, preferred_element_type=jnp.float32)
    features_out = summed_out.reshape(C, X, ZW, YW).astype(jnp.bfloat16)
    input_grad = summed_grad.reshape(C, X, ZW, YW).astype(jnp.bfloat16)
    return features_out, input_grad
```

```python
import functools

import jax
import jax.numpy as jnp
from jax import lax
from jax.experimental import pallas as pl
from jax.experimental.pallas import tpu as pltpu
from jax.sharding import PartitionSpec as P

MESH = pl.DeviceIdType.MESH


def with_halo(cells, sides, width):
    for axis, dim in sides:
        count = lax.axis_size(axis)
        head = lax.slice_in_dim(cells, 0, width, axis=dim)
        tail = lax.slice_in_dim(cells, cells.shape[dim] - width, cells.shape[dim], axis=dim)
        cells = jnp.concatenate(
            [
                lax.ppermute(tail, axis, [(i, (i + 1) % count) for i in range(count)]),
                cells,
                lax.ppermute(head, axis, [((i + 1) % count, i) for i in range(count)]),
            ],
            axis=dim,
        )
    return cells


def tap_sum(extended, weight, direction, pattern):
    planes = extended.shape[1] - 2
    depth = extended.shape[2]
    height = extended.shape[3]
    padded = jnp.pad(extended, ((0, 0), (0, 0), (1, 1), (1, 1)))
    summed = None
    for first in range(3):
        for second in range(3):
            for third in range(3):
                offset_x = 1 + direction * (first - 1)
                offset_y = 1 + direction * (second - 1)
                offset_z = 1 + direction * (third - 1)
                window_part = padded[
                    :,
                    offset_x : offset_x + planes,
                    offset_z : offset_z + depth,
                    offset_y : offset_y + height,
                ]
                product = jnp.einsum(
                    pattern,
                    window_part,
                    weight[9 * first + 3 * second + third],
                    preferred_element_type=jnp.float32,
                )
                summed = product if summed is None else summed + product
    return summed


def cell_faces(field):
    return with_halo(field, ((("gx", "ch"), 1),), 1)


def local_plain(activations, conv_weight, out_grad):
    full_weight = lax.all_gather(conv_weight, "ch", axis=2, tiled=True)
    cells_act, cells_grad = (
        lax.all_to_all(activations, "ch", split_axis=1, concat_axis=0, tiled=True),
        lax.all_to_all(out_grad, "ch", split_axis=1, concat_axis=0, tiled=True),
    )
    forward = tap_sum(cell_faces(cells_act), full_weight, 1, "kxzy,kn->nxzy").astype(jnp.bfloat16)
    backward = tap_sum(cell_faces(cells_grad), full_weight, -1, "kxzy,nk->nxzy").astype(
        jnp.bfloat16
    )
    return (
        lax.all_to_all(forward, "ch", split_axis=0, concat_axis=1, tiled=True),
        lax.all_to_all(backward, "ch", split_axis=0, concat_axis=1, tiled=True),
    )


def kernel(
    dims, act, grad, wsl, outf, outg,
    xa, xg, gathered, lf, lb, yf, yg,
    w1_send, w1_recv, w2_send, w2_recv, in_send, in_recv, halo_send, halo_recv,
    out_send, out_recv, own,
):
    n, m, rows, block, depth, height, taps = dims
    chans = m * rows
    per = wsl.shape[0]
    plane = depth * height
    span = block * plane
    g = lax.axis_index("gx")
    d = lax.axis_index("ch")

    def block_of(gg, dd):
        return jnp.where(lax.rem(gg, 2) == 0, dd, m - 1 - dd)

    k = block_of(g, d)

    def device_of(index):
        gg = lax.div(index, m)
        return gg, block_of(gg, lax.rem(index, m))

    whole = n * m
    spot = g * m + k
    prev = device_of(lax.rem(spot + whole - 1, whole))
    following = device_of(lax.rem(spot + 1, whole))

    def rows_at(dd):
        return pl.ds(pl.multiple_of(dd * rows, rows), rows)

    def cols_at(kk):
        return pl.ds(pl.multiple_of(kk * span, 128), span)

    barrier = pltpu.get_barrier_semaphore()
    for r in range(1, m):
        pl.semaphore_signal(barrier, inc=1, device_id=(g, lax.rem(d + r, m)), device_id_type=MESH)
    for r in range(1, n):
        pl.semaphore_signal(barrier, inc=1, device_id=(lax.rem(g + r, n), d), device_id_type=MESH)
    pl.semaphore_wait(barrier, m - 1 + n - 1)

    def remote(src, dst, send, recv, where):
        return pltpu.make_async_remote_copy(
            src_ref=src, dst_ref=dst, send_sem=send, recv_sem=recv,
            device_id=where, device_id_type=MESH,
        )

    mine = pl.ds(g * per, per)

    def w1(r, sending):
        dd = lax.rem(d + r, m) if sending else lax.rem(d + m - r, m)
        at = d if sending else dd
        return remote(wsl, gathered.at[mine, rows_at(at), :], w1_send.at[r], w1_recv.at[r], (g, dd))

    def w2(r, sending):
        gg = lax.rem(g + r, n) if sending else lax.rem(g + n - r, n)
        at = g if sending else gg
        part = gathered.at[pl.ds(at * per, per), :, :]
        return remote(part, part, w2_send.at[r], w2_recv.at[r], (gg, d))

    def spread(which, x, field, r, sending):
        dd = lax.rem(d + r, m) if sending else lax.rem(d + m - r, m)
        at = d if sending else dd
        return remote(
            field.at[:, cols_at(block_of(g, dd) if sending else k)],
            x.at[rows_at(at), pl.ds(plane, span)],
            in_send.at[which, r], in_recv.at[which, r], (g, dd),
        )

    def halo(which, x, side):
        first, last = pl.ds(plane, plane), pl.ds(span, plane)
        low, high = pl.ds(0, plane), pl.ds(span + plane, plane)
        src, dst, where = ((first, high, prev), (last, low, following))[side]
        return remote(
            x.at[:, src], x.at[:, dst], halo_send.at[which, side], halo_recv.at[which, side], where
        )

    def collect(which, y, out, r, sending):
        dd = lax.rem(d + r, m) if sending else lax.rem(d + m - r, m)
        at = k if sending else block_of(g, dd)
        return remote(
            y.at[rows_at(dd if sending else d), :], out.at[:, cols_at(at)],
            out_send.at[which, r], out_recv.at[which, r], (g, dd),
        )

    own_copies = [
        pltpu.make_async_copy(wsl, gathered.at[mine, rows_at(d), :], own.at[0]),
        pltpu.make_async_copy(act.at[:, cols_at(k)], xa.at[rows_at(d), pl.ds(plane, span)], own.at[1]),
        pltpu.make_async_copy(grad.at[:, cols_at(k)], xg.at[rows_at(d), pl.ds(plane, span)], own.at[2]),
    ]
    others, peers = range(1, m), range(1, n)
    for r in others:
        w1(r, True).start()
    for r in others:
        spread(0, xa, act, r, True).start()
    for c in own_copies:
        c.start()
    for c in own_copies:
        c.wait()
    for r in others:
        w1(r, False).wait_recv()

    @pl.when(g * per < taps)
    def _():
        for r in peers:
            w2(r, True).start()

    for r in others:
        spread(0, xa, act, r, True).wait_send()
    for r in others:
        spread(1, xg, grad, r, True).start()
    for r in others:
        spread(0, xa, act, r, False).wait_recv()
    for side in range(2):
        halo(0, xa, side).start()

    for r in peers:
        @pl.when(lax.rem(g + n - r, n) * per < taps)
        def _():
            w2(r, False).wait_recv()

    for a in range(3):
        for b in range(3):
            for c in range(3):
                at = pl.ds((3 * c + a) * chans, chans)
                lf[pl.ds(b * chans, chans), at] = gathered[9 * a + 3 * b + c]
                lb[pl.ds(b * chans, chans), at] = gathered[9 * (2 - a) + 3 * (2 - b) + 2 - c].T

    lane = lax.broadcasted_iota(jnp.int32, (chans, height), 1)

    def pair_sum(x, l, y, pair):
        def cells(slot, z):
            return x[:, pl.ds(slot * plane + z * height, height)]

        for z in range(depth):
            inside = [c for c in range(3) if 0 <= z + c - 1 < depth]
            right = jnp.concatenate(
                [
                    jnp.concatenate([cells(s + a - 1, z + c - 1) for s in pair], axis=1)
                    for c in inside
                    for a in range(3)
                ],
                axis=0,
            )
            left = l[:, pl.ds(inside[0] * 3 * chans, len(inside) * 3 * chans)]
            acc = jnp.dot(left, right, preferred_element_type=jnp.float32)
            for i, s in enumerate(pair):
                part = acc[:, i * height : (i + 1) * height]
                below = pltpu.roll(part[:chans], 1, 1)
                above = pltpu.roll(part[2 * chans :], height - 1, 1)
                total = (
                    part[chans : 2 * chans]
                    + jnp.where(lane > 0, below, 0.0)
                    + jnp.where(lane < height - 1, above, 0.0)
                )
                y[:, pl.ds((s - 1) * plane + z * height, height)] = total.astype(y.dtype)

    def finish(which, x, l, y, out):
        for s in range(2, block, 2):
            pair_sum(x, l, y, (s, s + 1))
        for side in range(2):
            halo(which, x, side).wait_recv()
        pair_sum(x, l, y, (1, block))
        for r in others:
            collect(which, y, out, r, True).start()
        copy = pltpu.make_async_copy(y.at[rows_at(d), :], out.at[:, cols_at(k)], own.at[3 + which])
        copy.start()
        return copy

    first_own = finish(0, xa, lf, yf, outf)
    for r in others:
        spread(1, xg, grad, r, False).wait_recv()
    for side in range(2):
        halo(1, xg, side).start()
    second_own = finish(1, xg, lb, yg, outg)

    first_own.wait()
    second_own.wait()
    for r in others:
        collect(0, yf, outf, r, False).wait_recv()
        collect(1, yg, outg, r, False).wait_recv()
        w1(r, True).wait_send()
        spread(1, xg, grad, r, True).wait_send()
        collect(0, yf, outf, r, True).wait_send()
        collect(1, yg, outg, r, True).wait_send()
    for which, x in ((0, xa), (1, xg)):
        for side in range(2):
            halo(which, x, side).wait_send()

    @pl.when(g * per < taps)
    def _():
        for r in peers:
            w2(r, True).wait_send()


def local_kernel(activations, conv_weight, out_grad):
    n, m = lax.axis_size("gx"), lax.axis_size("ch")
    rows, planes, depth, height = activations.shape
    taps, chans, _ = conv_weight.shape
    block = planes // m
    plane = depth * height
    per = -(-taps // n)
    padded = jnp.pad(conv_weight, ((0, per * n - taps), (0, 0), (0, 0)))
    wsl = lax.dynamic_slice_in_dim(padded, lax.axis_index("gx") * per, per, axis=0)
    wsl = jnp.swapaxes(wsl, 1, 2)
    vmem = pl.BlockSpec(memory_space=pltpu.VMEM)
    flat = jax.ShapeDtypeStruct((rows, planes * plane), jnp.bfloat16)
    sem = pltpu.SemaphoreType.DMA
    flops = 2 * 2 * taps * chans * chans * block * plane
    features, gradient = pl.pallas_call(
        functools.partial(kernel, (n, m, rows, block, depth, height, taps)),
        out_shape=(flat, flat),
        in_specs=[vmem] * 3,
        out_specs=(vmem, vmem),
        scratch_shapes=[
            pltpu.VMEM((chans, (block + 2) * plane), jnp.bfloat16),
            pltpu.VMEM((chans, (block + 2) * plane), jnp.bfloat16),
            pltpu.VMEM((per * n, chans, chans), jnp.bfloat16),
            pltpu.VMEM((3 * chans, 9 * chans), jnp.bfloat16),
            pltpu.VMEM((3 * chans, 9 * chans), jnp.bfloat16),
            pltpu.VMEM((chans, block * plane), jnp.bfloat16),
            pltpu.VMEM((chans, block * plane), jnp.bfloat16),
            sem((m,)), sem((m,)), sem((n,)), sem((n,)),
            sem((2, m)), sem((2, m)), sem((2, 2)), sem((2, 2)),
            sem((2, m)), sem((2, m)), sem((5,)),
        ],
        compiler_params=pltpu.CompilerParams(
            collective_id=0, has_side_effects=True, vmem_limit_bytes=40 * 2**20
        ),
        cost_estimate=pl.CostEstimate(
            flops=flops, bytes_accessed=8 * rows * planes * plane, transcendentals=0
        ),
    )(activations.reshape(rows, -1), out_grad.reshape(rows, -1), wsl)
    return features.reshape(activations.shape), gradient.reshape(out_grad.shape)


def local(activations, conv_weight, out_grad):
    n, m = lax.axis_size("gx"), lax.axis_size("ch")
    rows, planes, _, height = activations.shape
    fits = rows % 16 == 0 and planes % (2 * m) == 0 and height % 128 == 0 and n % 2 == 0
    plan = local_kernel if fits else local_plain
    return plan(activations, conv_weight, out_grad)


def solution(mesh):
    return jax.shard_map(
        local,
        mesh=mesh,
        in_specs=(P("ch", "gx", None, None), P(None, None, "ch"), P("ch", "gx", None, None)),
        out_specs=(P("ch", "gx", None, None), P("ch", "gx", None, None)),
        check_vma=False,
    )
```

```python
import functools

import jax
import jax.numpy as jnp
from jax import lax
from jax.experimental import pallas as pl
from jax.experimental.pallas import tpu as pltpu
from jax.sharding import PartitionSpec as P

MESH = pl.DeviceIdType.MESH


def with_halo(cells, sides, width):
    for axis, dim in sides:
        count = lax.axis_size(axis)
        head = lax.slice_in_dim(cells, 0, width, axis=dim)
        tail = lax.slice_in_dim(cells, cells.shape[dim] - width, cells.shape[dim], axis=dim)
        cells = jnp.concatenate(
            [
                lax.ppermute(tail, axis, [(i, (i + 1) % count) for i in range(count)]),
                cells,
                lax.ppermute(head, axis, [((i + 1) % count, i) for i in range(count)]),
            ],
            axis=dim,
        )
    return cells


def tap_sum(extended, weight, direction, pattern):
    planes = extended.shape[1] - 2
    depth = extended.shape[2]
    height = extended.shape[3]
    padded = jnp.pad(extended, ((0, 0), (0, 0), (1, 1), (1, 1)))
    summed = None
    for first in range(3):
        for second in range(3):
            for third in range(3):
                offset_x = 1 + direction * (first - 1)
                offset_y = 1 + direction * (second - 1)
                offset_z = 1 + direction * (third - 1)
                window_part = padded[
                    :,
                    offset_x : offset_x + planes,
                    offset_z : offset_z + depth,
                    offset_y : offset_y + height,
                ]
                product = jnp.einsum(
                    pattern,
                    window_part,
                    weight[9 * first + 3 * second + third],
                    preferred_element_type=jnp.float32,
                )
                summed = product if summed is None else summed + product
    return summed


def cell_faces(field):
    return with_halo(field, ((("gx", "ch"), 1),), 1)


def local_plain(activations, conv_weight, out_grad):
    full_weight = lax.all_gather(conv_weight, "ch", axis=2, tiled=True)
    cells_act, cells_grad = (
        lax.all_to_all(activations, "ch", split_axis=1, concat_axis=0, tiled=True),
        lax.all_to_all(out_grad, "ch", split_axis=1, concat_axis=0, tiled=True),
    )
    forward = tap_sum(cell_faces(cells_act), full_weight, 1, "kxzy,kn->nxzy").astype(jnp.bfloat16)
    backward = tap_sum(cell_faces(cells_grad), full_weight, -1, "kxzy,nk->nxzy").astype(
        jnp.bfloat16
    )
    return (
        lax.all_to_all(forward, "ch", split_axis=0, concat_axis=1, tiled=True),
        lax.all_to_all(backward, "ch", split_axis=0, concat_axis=1, tiled=True),
    )


def kernel(
    dims, act, grad, wsl, outf, outg,
    xa, xg, gathered, lf, lb, yf, yg,
    w1_send, w1_recv, w2_send, w2_recv, in_send, in_recv, halo_send, halo_recv,
    out_send, out_recv, extra_send, extra_recv, own,
):
    n, m, rows, block, depth, height, taps = dims
    chans = m * rows
    per = wsl.shape[0]
    plane = depth * height
    span = block * plane
    g = lax.axis_index("gx")
    d = lax.axis_index("ch")

    def block_of(gg, dd):
        return jnp.where(lax.rem(gg, 2) == 0, dd, m - 1 - dd)

    k = block_of(g, d)

    def device_of(index):
        gg = lax.div(index, m)
        return gg, block_of(gg, lax.rem(index, m))

    whole = n * m
    spot = g * m + k
    prev = device_of(lax.rem(spot + whole - 1, whole))
    following = device_of(lax.rem(spot + 1, whole))

    def rows_at(dd):
        return pl.ds(pl.multiple_of(dd * rows, rows), rows)

    def cols_at(kk):
        return pl.ds(pl.multiple_of(kk * span, 128), span)

    barrier = pltpu.get_barrier_semaphore()
    for r in range(1, m):
        pl.semaphore_signal(barrier, inc=1, device_id=(g, lax.rem(d + r, m)), device_id_type=MESH)
    for r in range(1, n):
        pl.semaphore_signal(barrier, inc=1, device_id=(lax.rem(g + r, n), d), device_id_type=MESH)
    pl.semaphore_wait(barrier, m - 1 + n - 1)

    def remote(src, dst, send, recv, where):
        return pltpu.make_async_remote_copy(
            src_ref=src, dst_ref=dst, send_sem=send, recv_sem=recv,
            device_id=where, device_id_type=MESH,
        )

    mine = pl.ds(g * per, per)

    def w1(r, sending):
        dd = lax.rem(d + r, m) if sending else lax.rem(d + m - r, m)
        at = d if sending else dd
        return remote(wsl, gathered.at[mine, rows_at(at), :], w1_send.at[r], w1_recv.at[r], (g, dd))

    def w2(r, sending):
        gg = lax.rem(g + r, n) if sending else lax.rem(g + n - r, n)
        at = g if sending else gg
        part = gathered.at[pl.ds(at * per, per), :, :]
        return remote(part, part, w2_send.at[r], w2_recv.at[r], (gg, d))

    def spread(which, x, field, r, sending):
        dd = lax.rem(d + r, m) if sending else lax.rem(d + m - r, m)
        at = d if sending else dd
        return remote(
            field.at[:, cols_at(block_of(g, dd) if sending else k)],
            x.at[rows_at(at), pl.ds(plane, span)],
            in_send.at[which, r], in_recv.at[which, r], (g, dd),
        )

    def middle(kk):
        return jnp.logical_or(kk == m // 2 - 1, kk == m // 2)

    def extra_cols(kk):
        upper = kk == m // 2
        src = jnp.where(upper, kk * span - plane, (kk + 1) * span)
        dst = jnp.where(upper, 0, span + plane)
        return pl.ds(pl.multiple_of(src, 128), plane), pl.ds(pl.multiple_of(dst, 128), plane)

    def extra(which, x, field, r, sending):
        dd = lax.rem(d + r, m) if sending else lax.rem(d + m - r, m)
        at = d if sending else dd
        src, dst = extra_cols(block_of(g, dd) if sending else k)
        return remote(
            field.at[:, src], x.at[rows_at(at), dst],
            extra_send.at[which, r], extra_recv.at[which, r], (g, dd),
        )

    def goes(r):
        return middle(block_of(g, lax.rem(d + r, m)))

    def spread_start(which, x, field, r):
        spread(which, x, field, r, True).start()

        @pl.when(goes(r))
        def _():
            extra(which, x, field, r, True).start()

    def spread_sent(which, x, field, r):
        spread(which, x, field, r, True).wait_send()

        @pl.when(goes(r))
        def _():
            extra(which, x, field, r, True).wait_send()

    def spread_landed(which, x, field):
        for r in others:
            spread(which, x, field, r, False).wait_recv()

        @pl.when(middle(k))
        def _():
            for r in others:
                extra(which, x, field, r, False).wait_recv()

    def halo(which, x, side):
        first, last = pl.ds(plane, plane), pl.ds(span, plane)
        low, high = pl.ds(0, plane), pl.ds(span + plane, plane)
        src, dst, where = ((first, high, prev), (last, low, following))[side]
        return remote(
            x.at[:, src], x.at[:, dst], halo_send.at[which, side], halo_recv.at[which, side], where
        )

    has_prev, has_next = k != m // 2, k != m // 2 - 1
    sends, lands = (has_prev, has_next), (has_next, has_prev)

    def halo_start(which, x):
        for side in range(2):
            @pl.when(sends[side])
            def _():
                halo(which, x, side).start()

    def halo_sent(which, x):
        for side in range(2):
            @pl.when(sends[side])
            def _():
                halo(which, x, side).wait_send()

    def halo_landed(which, x):
        for side in range(2):
            @pl.when(lands[side])
            def _():
                halo(which, x, side).wait_recv()

    pieces = [(0, plane), ((block - 1) * plane, plane)]
    if block > 2:
        pieces.append((plane, (block - 2) * plane))

    def collect(which, y, out, j, r, sending):
        dd = lax.rem(d + r, m) if sending else lax.rem(d + m - r, m)
        at = k if sending else block_of(g, dd)
        return remote(
            y.at[rows_at(dd if sending else d), pl.ds(*pieces[j])],
            out.at[:, pl.ds(pl.multiple_of(at * span + pieces[j][0], 128), pieces[j][1])],
            out_send.at[which, j, r], out_recv.at[which, j, r], (g, dd),
        )

    own_copies = [
        pltpu.make_async_copy(wsl, gathered.at[mine, rows_at(d), :], own.at[0]),
        pltpu.make_async_copy(act.at[:, cols_at(k)], xa.at[rows_at(d), pl.ds(plane, span)], own.at[1]),
        pltpu.make_async_copy(grad.at[:, cols_at(k)], xg.at[rows_at(d), pl.ds(plane, span)], own.at[2]),
    ]
    others, peers = range(1, m), range(1, n)
    even = lax.rem(d, 2) == 0
    order = [m // 2] + [
        r
        for i in range(1, m - m // 2)
        for r in (jnp.where(even, m // 2 + i, m // 2 - i), jnp.where(even, m // 2 - i, m // 2 + i))
    ]
    for r in order:
        w1(r, True).start()
    for r in order:
        spread_start(0, xa, act, r)
    for which, x, field in ((0, xa, act), (1, xg, grad)):
        @pl.when(middle(k))
        def _():
            src, dst = extra_cols(k)
            c = pltpu.make_async_copy(field.at[:, src], x.at[rows_at(d), dst], own.at[3 + which])
            c.start()
            c.wait()

    for c in own_copies:
        c.start()
    for c in own_copies:
        c.wait()
    for r in others:
        w1(r, False).wait_recv()

    @pl.when(g * per < taps)
    def _():
        for r in peers:
            w2(r, True).start()

    for r in order:
        spread_sent(0, xa, act, r)
        spread_start(1, xg, grad, r)
    spread_landed(0, xa, act)
    halo_start(0, xa)

    for r in peers:
        @pl.when(lax.rem(g + n - r, n) * per < taps)
        def _():
            w2(r, False).wait_recv()

    for a in range(3):
        for b in range(3):
            for c in range(3):
                at = pl.ds((3 * c + a) * chans, chans)
                lf[pl.ds(b * chans, chans), at] = gathered[9 * a + 3 * b + c]
                lb[pl.ds(b * chans, chans), at] = gathered[9 * (2 - a) + 3 * (2 - b) + 2 - c].T

    lane = lax.broadcasted_iota(jnp.int32, (chans, height), 1)

    def pair_sum(x, l, y, pair):
        def cells(slot, z):
            return x[:, pl.ds(slot * plane + z * height, height)]

        for z in range(depth):
            inside = [c for c in range(3) if 0 <= z + c - 1 < depth]
            right = jnp.concatenate(
                [
                    jnp.concatenate([cells(s + a - 1, z + c - 1) for s in pair], axis=1)
                    for c in inside
                    for a in range(3)
                ],
                axis=0,
            )
            left = l[:, pl.ds(inside[0] * 3 * chans, len(inside) * 3 * chans)]
            acc = jnp.dot(left, right, preferred_element_type=jnp.float32)
            for i, s in enumerate(pair):
                part = acc[:, i * height : (i + 1) * height]
                below = pltpu.roll(part[:chans], 1, 1)
                above = pltpu.roll(part[2 * chans :], height - 1, 1)
                total = (
                    part[chans : 2 * chans]
                    + jnp.where(lane > 0, below, 0.0)
                    + jnp.where(lane < height - 1, above, 0.0)
                )
                y[:, pl.ds((s - 1) * plane + z * height, height)] = total.astype(y.dtype)

    def finish(which, x, l, y, out):
        for s in range(2, block, 2):
            pair_sum(x, l, y, (s, s + 1))
        if block > 2:
            for r in order:
                collect(which, y, out, 2, r, True).start()
        halo_landed(which, x)
        pair_sum(x, l, y, (1, block))
        for r in order:
            for j in range(2):
                collect(which, y, out, j, r, True).start()
        copy = pltpu.make_async_copy(y.at[rows_at(d), :], out.at[:, cols_at(k)], own.at[3 + which])
        copy.start()
        return copy

    first_own = finish(0, xa, lf, yf, outf)
    spread_landed(1, xg, grad)
    halo_start(1, xg)
    second_own = finish(1, xg, lb, yg, outg)

    first_own.wait()
    second_own.wait()
    for r in others:
        w1(r, True).wait_send()
        spread_sent(1, xg, grad, r)
        for which, y, out in ((0, yf, outf), (1, yg, outg)):
            for j in range(len(pieces)):
                collect(which, y, out, j, r, False).wait_recv()
                collect(which, y, out, j, r, True).wait_send()
    halo_sent(0, xa)
    halo_sent(1, xg)

    @pl.when(g * per < taps)
    def _():
        for r in peers:
            w2(r, True).wait_send()


def local_kernel(activations, conv_weight, out_grad):
    n, m = lax.axis_size("gx"), lax.axis_size("ch")
    rows, planes, depth, height = activations.shape
    taps, chans, _ = conv_weight.shape
    block = planes // m
    plane = depth * height
    per = -(-taps // n)
    padded = jnp.pad(conv_weight, ((0, per * n - taps), (0, 0), (0, 0)))
    wsl = lax.dynamic_slice_in_dim(padded, lax.axis_index("gx") * per, per, axis=0)
    wsl = jnp.swapaxes(wsl, 1, 2)
    vmem = pl.BlockSpec(memory_space=pltpu.VMEM)
    flat = jax.ShapeDtypeStruct((rows, planes * plane), jnp.bfloat16)
    sem = pltpu.SemaphoreType.DMA
    flops = 2 * 2 * taps * chans * chans * block * plane
    features, gradient = pl.pallas_call(
        functools.partial(kernel, (n, m, rows, block, depth, height, taps)),
        out_shape=(flat, flat),
        in_specs=[vmem] * 3,
        out_specs=(vmem, vmem),
        scratch_shapes=[
            pltpu.VMEM((chans, (block + 2) * plane), jnp.bfloat16),
            pltpu.VMEM((chans, (block + 2) * plane), jnp.bfloat16),
            pltpu.VMEM((per * n, chans, chans), jnp.bfloat16),
            pltpu.VMEM((3 * chans, 9 * chans), jnp.bfloat16),
            pltpu.VMEM((3 * chans, 9 * chans), jnp.bfloat16),
            pltpu.VMEM((chans, block * plane), jnp.bfloat16),
            pltpu.VMEM((chans, block * plane), jnp.bfloat16),
            sem((m,)), sem((m,)), sem((n,)), sem((n,)),
            sem((2, m)), sem((2, m)), sem((2, 2)), sem((2, 2)),
            sem((2, 3, m)), sem((2, 3, m)), sem((2, m)), sem((2, m)), sem((5,)),
        ],
        compiler_params=pltpu.CompilerParams(
            collective_id=0, has_side_effects=True, vmem_limit_bytes=20 * 2**20
        ),
        cost_estimate=pl.CostEstimate(
            flops=flops, bytes_accessed=8 * rows * planes * plane, transcendentals=0
        ),
    )(activations.reshape(rows, -1), out_grad.reshape(rows, -1), wsl)
    return features.reshape(activations.shape), gradient.reshape(out_grad.shape)


def local(activations, conv_weight, out_grad):
    n, m = lax.axis_size("gx"), lax.axis_size("ch")
    rows, planes, _, height = activations.shape
    fits = rows % 16 == 0 and planes % (2 * m) == 0 and height % 128 == 0 and n % 2 == 0 and m % 2 == 0
    plan = local_kernel if fits else local_plain
    return plan(activations, conv_weight, out_grad)


def solution(mesh):
    return jax.shard_map(
        local,
        mesh=mesh,
        in_specs=(P("ch", "gx", None, None), P(None, None, "ch"), P("ch", "gx", None, None)),
        out_specs=(P("ch", "gx", None, None), P("ch", "gx", None, None)),
        check_vma=False,
    )
```

```python
import functools

import jax
import jax.numpy as jnp
from jax import lax
from jax.experimental import pallas as pl
from jax.experimental.pallas import tpu as pltpu
from jax.sharding import PartitionSpec as P

MESH = pl.DeviceIdType.MESH


def with_halo(cells, sides, width):
    for axis, dim in sides:
        count = lax.axis_size(axis)
        head = lax.slice_in_dim(cells, 0, width, axis=dim)
        tail = lax.slice_in_dim(cells, cells.shape[dim] - width, cells.shape[dim], axis=dim)
        cells = jnp.concatenate(
            [
                lax.ppermute(tail, axis, [(i, (i + 1) % count) for i in range(count)]),
                cells,
                lax.ppermute(head, axis, [((i + 1) % count, i) for i in range(count)]),
            ],
            axis=dim,
        )
    return cells


def tap_sum(extended, weight, direction, pattern):
    planes = extended.shape[1] - 2
    depth = extended.shape[2]
    height = extended.shape[3]
    padded = jnp.pad(extended, ((0, 0), (0, 0), (1, 1), (1, 1)))
    summed = None
    for first in range(3):
        for second in range(3):
            for third in range(3):
                offset_x = 1 + direction * (first - 1)
                offset_y = 1 + direction * (second - 1)
                offset_z = 1 + direction * (third - 1)
                window_part = padded[
                    :,
                    offset_x : offset_x + planes,
                    offset_z : offset_z + depth,
                    offset_y : offset_y + height,
                ]
                product = jnp.einsum(
                    pattern,
                    window_part,
                    weight[9 * first + 3 * second + third],
                    preferred_element_type=jnp.float32,
                )
                summed = product if summed is None else summed + product
    return summed


def cell_faces(field):
    return with_halo(field, ((("gx", "ch"), 1),), 1)


def local_plain(activations, conv_weight, out_grad):
    full_weight = lax.all_gather(conv_weight, "ch", axis=2, tiled=True)
    cells_act, cells_grad = (
        lax.all_to_all(activations, "ch", split_axis=1, concat_axis=0, tiled=True),
        lax.all_to_all(out_grad, "ch", split_axis=1, concat_axis=0, tiled=True),
    )
    forward = tap_sum(cell_faces(cells_act), full_weight, 1, "kxzy,kn->nxzy").astype(jnp.bfloat16)
    backward = tap_sum(cell_faces(cells_grad), full_weight, -1, "kxzy,nk->nxzy").astype(
        jnp.bfloat16
    )
    return (
        lax.all_to_all(forward, "ch", split_axis=0, concat_axis=1, tiled=True),
        lax.all_to_all(backward, "ch", split_axis=0, concat_axis=1, tiled=True),
    )


def kernel(
    dims, act_hbm, grad_hbm, weight_hbm, out_features, out_gradient,
    act_raw, grad_raw, act, grad, wsl, outf, outg,
    xa, xg, gathered, lf, lb, yf, yg,
    w1_send, w1_recv, w2_send, w2_recv, in_send, in_recv, halo_send, halo_recv,
    out_send, out_recv, extra_send, extra_recv, own, w_in,
):
    n, m, rows, block, depth, height, taps = dims
    chans = m * rows
    per = -(-taps // n)
    plane = depth * height
    span = block * plane
    g = lax.axis_index("gx")
    d = lax.axis_index("ch")

    def block_of(gg, dd):
        return jnp.where(lax.rem(gg, 2) == 0, dd, m - 1 - dd)

    k = block_of(g, d)

    def device_of(index):
        gg = lax.div(index, m)
        return gg, block_of(gg, lax.rem(index, m))

    whole = n * m
    spot = g * m + k
    prev = device_of(lax.rem(spot + whole - 1, whole))
    following = device_of(lax.rem(spot + 1, whole))

    def rows_at(dd):
        return pl.ds(pl.multiple_of(dd * rows, rows), rows)

    def cols_at(kk):
        return pl.ds(pl.multiple_of(kk * span, 128), span)

    loads = [
        pltpu.make_async_copy(act_hbm, act_raw, own.at[5]),
        pltpu.make_async_copy(grad_hbm, grad_raw, own.at[6]),
    ]
    taps_in = [
        pltpu.make_async_copy(
            weight_hbm.at[jnp.minimum(g * per + i, taps - 1)], wsl.at[i], w_in.at[i]
        )
        for i in range(per)
    ]
    loads[0].start()
    for c in taps_in:
        c.start()
    loads[1].start()

    barrier = pltpu.get_barrier_semaphore()
    for r in range(1, m):
        pl.semaphore_signal(barrier, inc=1, device_id=(g, lax.rem(d + r, m)), device_id_type=MESH)
    for r in range(1, n):
        pl.semaphore_signal(barrier, inc=1, device_id=(lax.rem(g + r, n), d), device_id_type=MESH)

    def flatten(raw, field):
        for p in range(block * m):
            field[:, pl.ds(p * plane, plane)] = raw[:, p].reshape(rows, plane)

    for c in taps_in:
        c.wait()
    loads[0].wait()
    flatten(act_raw, act)
    pl.semaphore_wait(barrier, m - 1 + n - 1)

    def remote(src, dst, send, recv, where):
        return pltpu.make_async_remote_copy(
            src_ref=src, dst_ref=dst, send_sem=send, recv_sem=recv,
            device_id=where, device_id_type=MESH,
        )

    mine = pl.ds(g * per, per)

    def w1(r, sending):
        dd = lax.rem(d + r, m) if sending else lax.rem(d + m - r, m)
        at = d if sending else dd
        return remote(wsl, gathered.at[mine, rows_at(at), :], w1_send.at[r], w1_recv.at[r], (g, dd))

    def w2(r, sending):
        gg = lax.rem(g + r, n) if sending else lax.rem(g + n - r, n)
        at = g if sending else gg
        part = gathered.at[pl.ds(at * per, per), :, :]
        return remote(part, part, w2_send.at[r], w2_recv.at[r], (gg, d))

    def spread(which, x, field, r, sending):
        dd = lax.rem(d + r, m) if sending else lax.rem(d + m - r, m)
        at = d if sending else dd
        return remote(
            field.at[:, cols_at(block_of(g, dd) if sending else k)],
            x.at[rows_at(at), pl.ds(plane, span)],
            in_send.at[which, r], in_recv.at[which, r], (g, dd),
        )

    def middle(kk):
        return jnp.logical_or(kk == m // 2 - 1, kk == m // 2)

    def extra_cols(kk):
        upper = kk == m // 2
        src = jnp.where(upper, kk * span - plane, (kk + 1) * span)
        dst = jnp.where(upper, 0, span + plane)
        return pl.ds(pl.multiple_of(src, 128), plane), pl.ds(pl.multiple_of(dst, 128), plane)

    def extra(which, x, field, r, sending):
        dd = lax.rem(d + r, m) if sending else lax.rem(d + m - r, m)
        at = d if sending else dd
        src, dst = extra_cols(block_of(g, dd) if sending else k)
        return remote(
            field.at[:, src], x.at[rows_at(at), dst],
            extra_send.at[which, r], extra_recv.at[which, r], (g, dd),
        )

    def goes(r):
        return middle(block_of(g, lax.rem(d + r, m)))

    def spread_start(which, x, field, r):
        spread(which, x, field, r, True).start()

        @pl.when(goes(r))
        def _():
            extra(which, x, field, r, True).start()

    def spread_sent(which, x, field, r):
        spread(which, x, field, r, True).wait_send()

        @pl.when(goes(r))
        def _():
            extra(which, x, field, r, True).wait_send()

    def spread_landed(which, x, field):
        for r in others:
            spread(which, x, field, r, False).wait_recv()

        @pl.when(middle(k))
        def _():
            for r in others:
                extra(which, x, field, r, False).wait_recv()

    def halo(which, x, side):
        first, last = pl.ds(plane, plane), pl.ds(span, plane)
        low, high = pl.ds(0, plane), pl.ds(span + plane, plane)
        src, dst, where = ((first, high, prev), (last, low, following))[side]
        return remote(
            x.at[:, src], x.at[:, dst], halo_send.at[which, side], halo_recv.at[which, side], where
        )

    has_prev, has_next = k != m // 2, k != m // 2 - 1
    sends, lands = (has_prev, has_next), (has_next, has_prev)

    def halo_start(which, x):
        for side in range(2):
            @pl.when(sends[side])
            def _():
                halo(which, x, side).start()

    def halo_sent(which, x):
        for side in range(2):
            @pl.when(sends[side])
            def _():
                halo(which, x, side).wait_send()

    def halo_landed(which, x):
        for side in range(2):
            @pl.when(lands[side])
            def _():
                halo(which, x, side).wait_recv()

    pieces = [(0, plane), ((block - 1) * plane, plane)]
    if block > 2:
        pieces.append((plane, (block - 2) * plane))

    def collect(which, y, out, j, r, sending):
        dd = lax.rem(d + r, m) if sending else lax.rem(d + m - r, m)
        at = k if sending else block_of(g, dd)
        return remote(
            y.at[rows_at(dd if sending else d), pl.ds(*pieces[j])],
            out.at[:, pl.ds(pl.multiple_of(at * span + pieces[j][0], 128), pieces[j][1])],
            out_send.at[which, j, r], out_recv.at[which, j, r], (g, dd),
        )

    own_copies = [
        pltpu.make_async_copy(wsl, gathered.at[mine, rows_at(d), :], own.at[0]),
        pltpu.make_async_copy(act.at[:, cols_at(k)], xa.at[rows_at(d), pl.ds(plane, span)], own.at[1]),
        pltpu.make_async_copy(grad.at[:, cols_at(k)], xg.at[rows_at(d), pl.ds(plane, span)], own.at[2]),
    ]
    others, peers = range(1, m), range(1, n)
    even = lax.rem(d, 2) == 0
    order = [m // 2] + [
        r
        for i in range(1, m - m // 2)
        for r in (jnp.where(even, m // 2 + i, m // 2 - i), jnp.where(even, m // 2 - i, m // 2 + i))
    ]
    for r in order:
        w1(r, True).start()
    for r in order:
        spread_start(0, xa, act, r)
    loads[1].wait()
    flatten(grad_raw, grad)
    for which, x, field in ((0, xa, act), (1, xg, grad)):
        @pl.when(middle(k))
        def _():
            src, dst = extra_cols(k)
            c = pltpu.make_async_copy(field.at[:, src], x.at[rows_at(d), dst], own.at[3 + which])
            c.start()
            c.wait()

    for c in own_copies:
        c.start()
    for c in own_copies:
        c.wait()
    for r in others:
        w1(r, False).wait_recv()

    @pl.when(g * per < taps)
    def _():
        for r in peers:
            w2(r, True).start()

    for r in order:
        spread_sent(0, xa, act, r)
        spread_start(1, xg, grad, r)
    spread_landed(0, xa, act)
    halo_start(0, xa)

    for r in peers:
        @pl.when(lax.rem(g + n - r, n) * per < taps)
        def _():
            w2(r, False).wait_recv()

    def filters(l, backward):
        for a in range(3):
            for b in range(3):
                for c in range(3):
                    tap = 9 * a + 3 * b + c
                    block_at = gathered[26 - tap].T if backward else gathered[tap]
                    l[pl.ds(b * chans, chans), pl.ds((3 * c + a) * chans, chans)] = block_at

    filters(lf, False)

    lane = lax.broadcasted_iota(jnp.int32, (chans, height), 1)

    def pair_sum(x, l, y, pair):
        def cells(slot, z):
            return x[:, pl.ds(slot * plane + z * height, height)]

        for z in range(depth):
            inside = [c for c in range(3) if 0 <= z + c - 1 < depth]
            right = jnp.concatenate(
                [
                    jnp.concatenate([cells(s + a - 1, z + c - 1) for s in pair], axis=1)
                    for c in inside
                    for a in range(3)
                ],
                axis=0,
            )
            left = l[:, pl.ds(inside[0] * 3 * chans, len(inside) * 3 * chans)]
            acc = jnp.dot(left, right, preferred_element_type=jnp.float32)
            for i, s in enumerate(pair):
                part = acc[:, i * height : (i + 1) * height]
                below = pltpu.roll(part[:chans], 1, 1)
                above = pltpu.roll(part[2 * chans :], height - 1, 1)
                total = (
                    part[chans : 2 * chans]
                    + jnp.where(lane > 0, below, 0.0)
                    + jnp.where(lane < height - 1, above, 0.0)
                )
                y[:, pl.ds((s - 1) * plane + z * height, height)] = total.astype(y.dtype)

    def finish(which, x, l, y, out):
        for s in range(2, block, 2):
            pair_sum(x, l, y, (s, s + 1))
        if block > 2:
            for r in order:
                collect(which, y, out, 2, r, True).start()
        halo_landed(which, x)
        pair_sum(x, l, y, (1, block))
        for r in order:
            for j in range(2):
                collect(which, y, out, j, r, True).start()
        copy = pltpu.make_async_copy(y.at[rows_at(d), :], out.at[:, cols_at(k)], own.at[3 + which])
        copy.start()
        return copy

    first_own = finish(0, xa, lf, yf, outf)
    filters(lb, True)
    spread_landed(1, xg, grad)
    halo_start(1, xg)
    second_own = finish(1, xg, lb, yg, outg)

    def unflatten(which, y, out, staged, result, own_copy):
        own_copy.wait()
        for r in others:
            for j in range(len(pieces)):
                collect(which, y, out, j, r, False).wait_recv()
        for p in range(block * m):
            staged[:, p] = out[:, pl.ds(p * plane, plane)].reshape(rows, depth, height)
        copy = pltpu.make_async_copy(staged, result, own.at[5 + which])
        copy.start()
        return copy

    stores = [
        unflatten(0, yf, outf, act_raw, out_features, first_own),
        unflatten(1, yg, outg, grad_raw, out_gradient, second_own),
    ]
    for r in others:
        w1(r, True).wait_send()
        spread_sent(1, xg, grad, r)
        for which, y, out in ((0, yf, outf), (1, yg, outg)):
            for j in range(len(pieces)):
                collect(which, y, out, j, r, True).wait_send()
    halo_sent(0, xa)
    halo_sent(1, xg)
    for c in stores:
        c.wait()

    @pl.when(g * per < taps)
    def _():
        for r in peers:
            w2(r, True).wait_send()


def local_kernel(activations, conv_weight, out_grad):
    n, m = lax.axis_size("gx"), lax.axis_size("ch")
    rows, planes, depth, height = activations.shape
    taps, chans, _ = conv_weight.shape
    block = planes // m
    plane = depth * height
    per = -(-taps // n)
    whole = jax.ShapeDtypeStruct(activations.shape, jnp.bfloat16)
    flat = pltpu.VMEM((rows, planes * plane), jnp.bfloat16)
    raw = pltpu.VMEM(activations.shape, jnp.bfloat16)
    sem = pltpu.SemaphoreType.DMA
    flops = 2 * 2 * taps * chans * chans * block * plane
    features, gradient = pl.pallas_call(
        functools.partial(kernel, (n, m, rows, block, depth, height, taps)),
        out_shape=(whole, whole),
        in_specs=[pl.BlockSpec(memory_space=pl.ANY)] * 3,
        out_specs=(pl.BlockSpec(memory_space=pl.ANY),) * 2,
        scratch_shapes=[
            raw,
            raw,
            flat,
            flat,
            pltpu.VMEM((per, rows, chans), jnp.bfloat16),
            flat,
            flat,
            pltpu.VMEM((chans, (block + 2) * plane), jnp.bfloat16),
            pltpu.VMEM((chans, (block + 2) * plane), jnp.bfloat16),
            pltpu.VMEM((per * n, chans, chans), jnp.bfloat16),
            pltpu.VMEM((3 * chans, 9 * chans), jnp.bfloat16),
            pltpu.VMEM((3 * chans, 9 * chans), jnp.bfloat16),
            pltpu.VMEM((chans, block * plane), jnp.bfloat16),
            pltpu.VMEM((chans, block * plane), jnp.bfloat16),
            sem((m,)), sem((m,)), sem((n,)), sem((n,)),
            sem((2, m)), sem((2, m)), sem((2, 2)), sem((2, 2)),
            sem((2, 3, m)), sem((2, 3, m)), sem((2, m)), sem((2, m)), sem((7,)), sem((per,)),
        ],
        compiler_params=pltpu.CompilerParams(
            collective_id=0, has_side_effects=True, vmem_limit_bytes=60 * 2**20
        ),
        cost_estimate=pl.CostEstimate(
            flops=flops, bytes_accessed=8 * rows * planes * plane, transcendentals=0
        ),
    )(activations, out_grad, jnp.swapaxes(conv_weight, 1, 2))
    return features, gradient


def local(activations, conv_weight, out_grad):
    n, m = lax.axis_size("gx"), lax.axis_size("ch")
    rows, planes, _, height = activations.shape
    fits = rows % 16 == 0 and planes % (2 * m) == 0 and height % 128 == 0 and n % 2 == 0 and m % 2 == 0
    plan = local_kernel if fits else local_plain
    return plan(activations, conv_weight, out_grad)


def solution(mesh):
    return jax.shard_map(
        local,
        mesh=mesh,
        in_specs=(P("ch", "gx", None, None), P(None, None, "ch"), P("ch", "gx", None, None)),
        out_specs=(P("ch", "gx", None, None), P("ch", "gx", None, None)),
        check_vma=False,
    )
```

```python
import functools

import jax
import jax.numpy as jnp
from jax import lax
from jax.experimental import pallas as pl
from jax.experimental.pallas import tpu as pltpu
from jax.sharding import PartitionSpec as P

MESH = pl.DeviceIdType.MESH


def with_halo(cells, sides, width):
    for axis, dim in sides:
        count = lax.axis_size(axis)
        head = lax.slice_in_dim(cells, 0, width, axis=dim)
        tail = lax.slice_in_dim(cells, cells.shape[dim] - width, cells.shape[dim], axis=dim)
        cells = jnp.concatenate(
            [
                lax.ppermute(tail, axis, [(i, (i + 1) % count) for i in range(count)]),
                cells,
                lax.ppermute(head, axis, [((i + 1) % count, i) for i in range(count)]),
            ],
            axis=dim,
        )
    return cells


def tap_sum(extended, weight, direction, pattern):
    planes = extended.shape[1] - 2
    depth = extended.shape[2]
    height = extended.shape[3]
    padded = jnp.pad(extended, ((0, 0), (0, 0), (1, 1), (1, 1)))
    summed = None
    for first in range(3):
        for second in range(3):
            for third in range(3):
                offset_x = 1 + direction * (first - 1)
                offset_y = 1 + direction * (second - 1)
                offset_z = 1 + direction * (third - 1)
                window_part = padded[
                    :,
                    offset_x : offset_x + planes,
                    offset_z : offset_z + depth,
                    offset_y : offset_y + height,
                ]
                product = jnp.einsum(
                    pattern,
                    window_part,
                    weight[9 * first + 3 * second + third],
                    preferred_element_type=jnp.float32,
                )
                summed = product if summed is None else summed + product
    return summed


def cell_faces(field):
    return with_halo(field, ((("gx", "ch"), 1),), 1)


def local_plain(activations, conv_weight, out_grad):
    full_weight = lax.all_gather(conv_weight, "ch", axis=2, tiled=True)
    cells_act, cells_grad = (
        lax.all_to_all(activations, "ch", split_axis=1, concat_axis=0, tiled=True),
        lax.all_to_all(out_grad, "ch", split_axis=1, concat_axis=0, tiled=True),
    )
    forward = tap_sum(cell_faces(cells_act), full_weight, 1, "kxzy,kn->nxzy").astype(jnp.bfloat16)
    backward = tap_sum(cell_faces(cells_grad), full_weight, -1, "kxzy,nk->nxzy").astype(
        jnp.bfloat16
    )
    return (
        lax.all_to_all(forward, "ch", split_axis=0, concat_axis=1, tiled=True),
        lax.all_to_all(backward, "ch", split_axis=0, concat_axis=1, tiled=True),
    )


def kernel(
    dims, act_raw, grad_raw, weight, out_features, out_gradient,
    act, grad, wsl, outf, outg,
    xa, xg, gathered, lf, lb, yf, yg,
    w1_send, w1_recv, w2_send, w2_recv, in_send, in_recv, halo_send, halo_recv,
    out_send, out_recv, extra_send, extra_recv, own,
):
    n, m, rows, block, depth, height, taps = dims
    chans = m * rows
    per = -(-taps // n)
    plane = depth * height
    span = block * plane
    g = lax.axis_index("gx")
    d = lax.axis_index("ch")

    def block_of(gg, dd):
        return jnp.where(lax.rem(gg, 2) == 0, dd, m - 1 - dd)

    k = block_of(g, d)

    def device_of(index):
        gg = lax.div(index, m)
        return gg, block_of(gg, lax.rem(index, m))

    whole = n * m
    spot = g * m + k
    prev = device_of(lax.rem(spot + whole - 1, whole))
    following = device_of(lax.rem(spot + 1, whole))

    def rows_at(dd):
        return pl.ds(pl.multiple_of(dd * rows, rows), rows)

    def cols_at(kk):
        return pl.ds(pl.multiple_of(kk * span, 128), span)

    barrier = pltpu.get_barrier_semaphore()
    for r in range(1, m):
        pl.semaphore_signal(barrier, inc=1, device_id=(g, lax.rem(d + r, m)), device_id_type=MESH)
    for r in range(1, n):
        pl.semaphore_signal(barrier, inc=1, device_id=(lax.rem(g + r, n), d), device_id_type=MESH)

    def flatten(raw, field):
        for p in range(block * m):
            field[:, pl.ds(p * plane, plane)] = raw[:, p].reshape(rows, plane)

    for i in range(per):
        wsl[i] = weight[jnp.minimum(g * per + i, taps - 1)]
    flatten(act_raw, act)
    pl.semaphore_wait(barrier, m - 1 + n - 1)

    def remote(src, dst, send, recv, where):
        return pltpu.make_async_remote_copy(
            src_ref=src, dst_ref=dst, send_sem=send, recv_sem=recv,
            device_id=where, device_id_type=MESH,
        )

    mine = pl.ds(g * per, per)

    def w1(r, sending):
        dd = lax.rem(d + r, m) if sending else lax.rem(d + m - r, m)
        at = d if sending else dd
        return remote(wsl, gathered.at[mine, rows_at(at), :], w1_send.at[r], w1_recv.at[r], (g, dd))

    def w2(r, sending):
        gg = lax.rem(g + r, n) if sending else lax.rem(g + n - r, n)
        at = g if sending else gg
        part = gathered.at[pl.ds(at * per, per), :, :]
        return remote(part, part, w2_send.at[r], w2_recv.at[r], (gg, d))

    def spread(which, x, field, r, sending):
        dd = lax.rem(d + r, m) if sending else lax.rem(d + m - r, m)
        at = d if sending else dd
        return remote(
            field.at[:, cols_at(block_of(g, dd) if sending else k)],
            x.at[rows_at(at), pl.ds(plane, span)],
            in_send.at[which, r], in_recv.at[which, r], (g, dd),
        )

    def middle(kk):
        return jnp.logical_or(kk == m // 2 - 1, kk == m // 2)

    def extra_cols(kk):
        upper = kk == m // 2
        src = jnp.where(upper, kk * span - plane, (kk + 1) * span)
        dst = jnp.where(upper, 0, span + plane)
        return pl.ds(pl.multiple_of(src, 128), plane), pl.ds(pl.multiple_of(dst, 128), plane)

    def extra(which, x, field, r, sending):
        dd = lax.rem(d + r, m) if sending else lax.rem(d + m - r, m)
        at = d if sending else dd
        src, dst = extra_cols(block_of(g, dd) if sending else k)
        return remote(
            field.at[:, src], x.at[rows_at(at), dst],
            extra_send.at[which, r], extra_recv.at[which, r], (g, dd),
        )

    def goes(r):
        return middle(block_of(g, lax.rem(d + r, m)))

    def spread_start(which, x, field, r):
        spread(which, x, field, r, True).start()

        @pl.when(goes(r))
        def _():
            extra(which, x, field, r, True).start()

    def spread_sent(which, x, field, r):
        spread(which, x, field, r, True).wait_send()

        @pl.when(goes(r))
        def _():
            extra(which, x, field, r, True).wait_send()

    def spread_landed(which, x, field):
        for r in others:
            spread(which, x, field, r, False).wait_recv()

        @pl.when(middle(k))
        def _():
            for r in others:
                extra(which, x, field, r, False).wait_recv()

    def halo(which, x, side):
        first, last = pl.ds(plane, plane), pl.ds(span, plane)
        low, high = pl.ds(0, plane), pl.ds(span + plane, plane)
        src, dst, where = ((first, high, prev), (last, low, following))[side]
        return remote(
            x.at[:, src], x.at[:, dst], halo_send.at[which, side], halo_recv.at[which, side], where
        )

    has_prev, has_next = k != m // 2, k != m // 2 - 1
    sends, lands = (has_prev, has_next), (has_next, has_prev)

    def halo_start(which, x):
        for side in range(2):
            @pl.when(sends[side])
            def _():
                halo(which, x, side).start()

    def halo_sent(which, x):
        for side in range(2):
            @pl.when(sends[side])
            def _():
                halo(which, x, side).wait_send()

    def halo_landed(which, x):
        for side in range(2):
            @pl.when(lands[side])
            def _():
                halo(which, x, side).wait_recv()

    pieces = [(0, plane), ((block - 1) * plane, plane)]
    if block > 2:
        pieces.append((plane, (block - 2) * plane))

    def collect(which, y, out, j, r, sending):
        dd = lax.rem(d + r, m) if sending else lax.rem(d + m - r, m)
        at = k if sending else block_of(g, dd)
        return remote(
            y.at[rows_at(dd if sending else d), pl.ds(*pieces[j])],
            out.at[:, pl.ds(pl.multiple_of(at * span + pieces[j][0], 128), pieces[j][1])],
            out_send.at[which, j, r], out_recv.at[which, j, r], (g, dd),
        )

    own_copies = [
        pltpu.make_async_copy(wsl, gathered.at[mine, rows_at(d), :], own.at[0]),
        pltpu.make_async_copy(act.at[:, cols_at(k)], xa.at[rows_at(d), pl.ds(plane, span)], own.at[1]),
        pltpu.make_async_copy(grad.at[:, cols_at(k)], xg.at[rows_at(d), pl.ds(plane, span)], own.at[2]),
    ]
    others, peers = range(1, m), range(1, n)
    even = lax.rem(d, 2) == 0
    order = [m // 2] + [
        r
        for i in range(1, m - m // 2)
        for r in (jnp.where(even, m // 2 + i, m // 2 - i), jnp.where(even, m // 2 - i, m // 2 + i))
    ]
    for r in order:
        w1(r, True).start()
    for r in order:
        spread_start(0, xa, act, r)
    flatten(grad_raw, grad)
    for which, x, field in ((0, xa, act), (1, xg, grad)):
        @pl.when(middle(k))
        def _():
            src, dst = extra_cols(k)
            c = pltpu.make_async_copy(field.at[:, src], x.at[rows_at(d), dst], own.at[3 + which])
            c.start()
            c.wait()

    for c in own_copies:
        c.start()
    for c in own_copies:
        c.wait()
    for r in others:
        w1(r, False).wait_recv()

    @pl.when(g * per < taps)
    def _():
        for r in peers:
            w2(r, True).start()

    for r in order:
        spread_sent(0, xa, act, r)
        spread_start(1, xg, grad, r)
    spread_landed(0, xa, act)
    halo_start(0, xa)

    for r in peers:
        @pl.when(lax.rem(g + n - r, n) * per < taps)
        def _():
            w2(r, False).wait_recv()

    def filters(l, backward):
        for a in range(3):
            for b in range(3):
                for c in range(3):
                    tap = 9 * a + 3 * b + c
                    block_at = gathered[26 - tap].T if backward else gathered[tap]
                    l[pl.ds(b * chans, chans), pl.ds((3 * c + a) * chans, chans)] = block_at

    filters(lf, False)

    lane = lax.broadcasted_iota(jnp.int32, (chans, height), 1)

    def pair_sum(x, l, y, pair):
        def cells(slot, z):
            return x[:, pl.ds(slot * plane + z * height, height)]

        for z in range(depth):
            inside = [c for c in range(3) if 0 <= z + c - 1 < depth]
            right = jnp.concatenate(
                [
                    jnp.concatenate([cells(s + a - 1, z + c - 1) for s in pair], axis=1)
                    for c in inside
                    for a in range(3)
                ],
                axis=0,
            )
            left = l[:, pl.ds(inside[0] * 3 * chans, len(inside) * 3 * chans)]
            acc = jnp.dot(left, right, preferred_element_type=jnp.float32)
            for i, s in enumerate(pair):
                part = acc[:, i * height : (i + 1) * height]
                below = pltpu.roll(part[:chans], 1, 1)
                above = pltpu.roll(part[2 * chans :], height - 1, 1)
                total = (
                    part[chans : 2 * chans]
                    + jnp.where(lane > 0, below, 0.0)
                    + jnp.where(lane < height - 1, above, 0.0)
                )
                y[:, pl.ds((s - 1) * plane + z * height, height)] = total.astype(y.dtype)

    def finish(which, x, l, y, out):
        for s in range(2, block, 2):
            pair_sum(x, l, y, (s, s + 1))
        if block > 2:
            for r in order:
                collect(which, y, out, 2, r, True).start()
        halo_landed(which, x)
        pair_sum(x, l, y, (1, block))
        for r in order:
            for j in range(2):
                collect(which, y, out, j, r, True).start()
        copy = pltpu.make_async_copy(y.at[rows_at(d), :], out.at[:, cols_at(k)], own.at[3 + which])
        copy.start()
        return copy

    first_own = finish(0, xa, lf, yf, outf)
    filters(lb, True)
    spread_landed(1, xg, grad)
    halo_start(1, xg)
    second_own = finish(1, xg, lb, yg, outg)

    def unflatten(which, y, out, result, own_copy):
        own_copy.wait()
        for r in others:
            for j in range(len(pieces)):
                collect(which, y, out, j, r, False).wait_recv()
        for p in range(block * m):
            result[:, p] = out[:, pl.ds(p * plane, plane)].reshape(rows, depth, height)

    unflatten(0, yf, outf, out_features, first_own)
    unflatten(1, yg, outg, out_gradient, second_own)
    for r in others:
        w1(r, True).wait_send()
        spread_sent(1, xg, grad, r)
        for which, y, out in ((0, yf, outf), (1, yg, outg)):
            for j in range(len(pieces)):
                collect(which, y, out, j, r, True).wait_send()
    halo_sent(0, xa)
    halo_sent(1, xg)

    @pl.when(g * per < taps)
    def _():
        for r in peers:
            w2(r, True).wait_send()


def store(features, gradient, out_features, out_gradient, sems):
    copies = [
        pltpu.make_async_copy(features, out_features, sems.at[0]),
        pltpu.make_async_copy(gradient, out_gradient, sems.at[1]),
    ]
    for c in copies:
        c.start()
    for c in copies:
        c.wait()


def local_kernel(activations, conv_weight, out_grad):
    n, m = lax.axis_size("gx"), lax.axis_size("ch")
    rows, planes, depth, height = activations.shape
    taps, chans, _ = conv_weight.shape
    block = planes // m
    plane = depth * height
    per = -(-taps // n)
    whole = jax.ShapeDtypeStruct(activations.shape, jnp.bfloat16)
    flat = pltpu.VMEM((rows, planes * plane), jnp.bfloat16)
    vmem = pl.BlockSpec(memory_space=pltpu.VMEM)
    hbm = pl.BlockSpec(memory_space=pl.ANY)
    sem = pltpu.SemaphoreType.DMA
    flops = 2 * 2 * taps * chans * chans * block * plane
    features, gradient = pl.pallas_call(
        functools.partial(kernel, (n, m, rows, block, depth, height, taps)),
        out_shape=(whole, whole),
        in_specs=[vmem] * 3,
        out_specs=(vmem, vmem),
        scratch_shapes=[
            flat,
            flat,
            pltpu.VMEM((per, rows, chans), jnp.bfloat16),
            flat,
            flat,
            pltpu.VMEM((chans, (block + 2) * plane), jnp.bfloat16),
            pltpu.VMEM((chans, (block + 2) * plane), jnp.bfloat16),
            pltpu.VMEM((per * n, chans, chans), jnp.bfloat16),
            pltpu.VMEM((3 * chans, 9 * chans), jnp.bfloat16),
            pltpu.VMEM((3 * chans, 9 * chans), jnp.bfloat16),
            pltpu.VMEM((chans, block * plane), jnp.bfloat16),
            pltpu.VMEM((chans, block * plane), jnp.bfloat16),
            sem((m,)), sem((m,)), sem((n,)), sem((n,)),
            sem((2, m)), sem((2, m)), sem((2, 2)), sem((2, 2)),
            sem((2, 3, m)), sem((2, 3, m)), sem((2, m)), sem((2, m)), sem((5,)),
        ],
        compiler_params=pltpu.CompilerParams(
            collective_id=0, has_side_effects=True, vmem_limit_bytes=28 * 2**20
        ),
        cost_estimate=pl.CostEstimate(
            flops=flops, bytes_accessed=8 * rows * planes * plane, transcendentals=0
        ),
    )(activations, out_grad, jnp.swapaxes(conv_weight, 1, 2))
    return pl.pallas_call(
        store,
        out_shape=(whole, whole),
        in_specs=[vmem] * 2,
        out_specs=(hbm, hbm),
        scratch_shapes=[sem((2,))],
    )(features, gradient)


def local(activations, conv_weight, out_grad):
    n, m = lax.axis_size("gx"), lax.axis_size("ch")
    rows, planes, _, height = activations.shape
    fits = rows % 16 == 0 and planes % (2 * m) == 0 and height % 128 == 0 and n % 2 == 0 and m % 2 == 0
    plan = local_kernel if fits else local_plain
    return plan(activations, conv_weight, out_grad)


def solution(mesh):
    return jax.shard_map(
        local,
        mesh=mesh,
        in_specs=(P("ch", "gx", None, None), P(None, None, "ch"), P("ch", "gx", None, None)),
        out_specs=(P("ch", "gx", None, None), P("ch", "gx", None, None)),
        check_vma=False,
    )
```

```python
import functools

import jax
import jax.numpy as jnp
from jax import lax
from jax.experimental import pallas as pl
from jax.experimental.pallas import tpu as pltpu
from jax.sharding import PartitionSpec as P

MESH = pl.DeviceIdType.MESH


def with_halo(cells, sides, width):
    for axis, dim in sides:
        count = lax.axis_size(axis)
        head = lax.slice_in_dim(cells, 0, width, axis=dim)
        tail = lax.slice_in_dim(cells, cells.shape[dim] - width, cells.shape[dim], axis=dim)
        cells = jnp.concatenate(
            [
                lax.ppermute(tail, axis, [(i, (i + 1) % count) for i in range(count)]),
                cells,
                lax.ppermute(head, axis, [((i + 1) % count, i) for i in range(count)]),
            ],
            axis=dim,
        )
    return cells


def tap_sum(extended, weight, direction, pattern):
    planes = extended.shape[1] - 2
    depth = extended.shape[2]
    height = extended.shape[3]
    padded = jnp.pad(extended, ((0, 0), (0, 0), (1, 1), (1, 1)))
    summed = None
    for first in range(3):
        for second in range(3):
            for third in range(3):
                offset_x = 1 + direction * (first - 1)
                offset_y = 1 + direction * (second - 1)
                offset_z = 1 + direction * (third - 1)
                window_part = padded[
                    :,
                    offset_x : offset_x + planes,
                    offset_z : offset_z + depth,
                    offset_y : offset_y + height,
                ]
                product = jnp.einsum(
                    pattern,
                    window_part,
                    weight[9 * first + 3 * second + third],
                    preferred_element_type=jnp.float32,
                )
                summed = product if summed is None else summed + product
    return summed


def cell_faces(field):
    return with_halo(field, ((("gx", "ch"), 1),), 1)


def local_plain(activations, conv_weight, out_grad):
    full_weight = lax.all_gather(conv_weight, "ch", axis=2, tiled=True)
    cells_act, cells_grad = (
        lax.all_to_all(activations, "ch", split_axis=1, concat_axis=0, tiled=True),
        lax.all_to_all(out_grad, "ch", split_axis=1, concat_axis=0, tiled=True),
    )
    forward = tap_sum(cell_faces(cells_act), full_weight, 1, "kxzy,kn->nxzy").astype(jnp.bfloat16)
    backward = tap_sum(cell_faces(cells_grad), full_weight, -1, "kxzy,nk->nxzy").astype(
        jnp.bfloat16
    )
    return (
        lax.all_to_all(forward, "ch", split_axis=0, concat_axis=1, tiled=True),
        lax.all_to_all(backward, "ch", split_axis=0, concat_axis=1, tiled=True),
    )


def kernel(
    dims, act_hbm, grad_hbm, weight_hbm, out_features, out_gradient,
    act_raw, grad_raw, act, grad, wsl, outf, outg,
    xa, xg, gathered, lf, lb, yf, yg,
    w1_send, w1_recv, w2_send, w2_recv, in_send, in_recv, halo_send, halo_recv,
    out_send, out_recv, extra_send, extra_recv, own, w_in, loaded,
):
    n, m, rows, block, depth, height, taps = dims
    chans = m * rows
    per = -(-taps // n)
    plane = depth * height
    span = block * plane
    g = lax.axis_index("gx")
    d = lax.axis_index("ch")

    def block_of(gg, dd):
        return jnp.where(lax.rem(gg, 2) == 0, dd, m - 1 - dd)

    k = block_of(g, d)

    def device_of(index):
        gg = lax.div(index, m)
        return gg, block_of(gg, lax.rem(index, m))

    whole = n * m
    spot = g * m + k
    prev = device_of(lax.rem(spot + whole - 1, whole))
    following = device_of(lax.rem(spot + 1, whole))

    def rows_at(dd):
        return pl.ds(pl.multiple_of(dd * rows, rows), rows)

    def cols_at(kk):
        return pl.ds(pl.multiple_of(kk * span, 128), span)

    cut = rows // 8
    loads = [
        [
            pltpu.make_async_copy(
                src.at[pl.ds(i * cut, cut)], dst.at[pl.ds(i * cut, cut)], loaded.at[which, i]
            )
            for i in range(8)
        ]
        for which, (src, dst) in enumerate(((act_hbm, act_raw), (grad_hbm, grad_raw)))
    ]
    taps_in = [
        pltpu.make_async_copy(
            weight_hbm.at[jnp.minimum(g * per + i, taps - 1)], wsl.at[i], w_in.at[i]
        )
        for i in range(per)
    ]
    for c in loads[0]:
        c.start()
    for c in taps_in:
        c.start()
    for c in loads[1]:
        c.start()

    barrier = pltpu.get_barrier_semaphore()
    for r in range(1, m):
        pl.semaphore_signal(barrier, inc=1, device_id=(g, lax.rem(d + r, m)), device_id_type=MESH)
    for r in range(1, n):
        pl.semaphore_signal(barrier, inc=1, device_id=(lax.rem(g + r, n), d), device_id_type=MESH)

    def flatten(raw, field):
        for p in range(block * m):
            field[:, pl.ds(p * plane, plane)] = raw[:, p].reshape(rows, plane)

    for c in taps_in:
        c.wait()
    for c in loads[0]:
        c.wait()
    flatten(act_raw, act)
    pl.semaphore_wait(barrier, m - 1 + n - 1)

    def remote(src, dst, send, recv, where):
        return pltpu.make_async_remote_copy(
            src_ref=src, dst_ref=dst, send_sem=send, recv_sem=recv,
            device_id=where, device_id_type=MESH,
        )

    mine = pl.ds(g * per, per)

    def w1(r, sending):
        dd = lax.rem(d + r, m) if sending else lax.rem(d + m - r, m)
        at = d if sending else dd
        return remote(wsl, gathered.at[mine, rows_at(at), :], w1_send.at[r], w1_recv.at[r], (g, dd))

    def w2(r, sending):
        gg = lax.rem(g + r, n) if sending else lax.rem(g + n - r, n)
        at = g if sending else gg
        part = gathered.at[pl.ds(at * per, per), :, :]
        return remote(part, part, w2_send.at[r], w2_recv.at[r], (gg, d))

    def spread(which, x, field, r, sending):
        dd = lax.rem(d + r, m) if sending else lax.rem(d + m - r, m)
        at = d if sending else dd
        return remote(
            field.at[:, cols_at(block_of(g, dd) if sending else k)],
            x.at[rows_at(at), pl.ds(plane, span)],
            in_send.at[which, r], in_recv.at[which, r], (g, dd),
        )

    def middle(kk):
        return jnp.logical_or(kk == m // 2 - 1, kk == m // 2)

    def extra_cols(kk):
        upper = kk == m // 2
        src = jnp.where(upper, kk * span - plane, (kk + 1) * span)
        dst = jnp.where(upper, 0, span + plane)
        return pl.ds(pl.multiple_of(src, 128), plane), pl.ds(pl.multiple_of(dst, 128), plane)

    def extra(which, x, field, r, sending):
        dd = lax.rem(d + r, m) if sending else lax.rem(d + m - r, m)
        at = d if sending else dd
        src, dst = extra_cols(block_of(g, dd) if sending else k)
        return remote(
            field.at[:, src], x.at[rows_at(at), dst],
            extra_send.at[which, r], extra_recv.at[which, r], (g, dd),
        )

    def goes(r):
        return middle(block_of(g, lax.rem(d + r, m)))

    def spread_start(which, x, field, r):
        spread(which, x, field, r, True).start()

        @pl.when(goes(r))
        def _():
            extra(which, x, field, r, True).start()

    def spread_sent(which, x, field, r):
        spread(which, x, field, r, True).wait_send()

        @pl.when(goes(r))
        def _():
            extra(which, x, field, r, True).wait_send()

    def spread_landed(which, x, field):
        for r in others:
            spread(which, x, field, r, False).wait_recv()

        @pl.when(middle(k))
        def _():
            for r in others:
                extra(which, x, field, r, False).wait_recv()

    def halo(which, x, side):
        first, last = pl.ds(plane, plane), pl.ds(span, plane)
        low, high = pl.ds(0, plane), pl.ds(span + plane, plane)
        src, dst, where = ((first, high, prev), (last, low, following))[side]
        return remote(
            x.at[:, src], x.at[:, dst], halo_send.at[which, side], halo_recv.at[which, side], where
        )

    has_prev, has_next = k != m // 2, k != m // 2 - 1
    sends, lands = (has_prev, has_next), (has_next, has_prev)

    def halo_start(which, x):
        for side in range(2):
            @pl.when(sends[side])
            def _():
                halo(which, x, side).start()

    def halo_sent(which, x):
        for side in range(2):
            @pl.when(sends[side])
            def _():
                halo(which, x, side).wait_send()

    def halo_landed(which, x):
        for side in range(2):
            @pl.when(lands[side])
            def _():
                halo(which, x, side).wait_recv()

    pieces = [(0, plane), ((block - 1) * plane, plane)]
    if block > 2:
        pieces.append((plane, (block - 2) * plane))

    def collect(which, y, out, j, r, sending):
        dd = lax.rem(d + r, m) if sending else lax.rem(d + m - r, m)
        at = k if sending else block_of(g, dd)
        return remote(
            y.at[rows_at(dd if sending else d), pl.ds(*pieces[j])],
            out.at[:, pl.ds(pl.multiple_of(at * span + pieces[j][0], 128), pieces[j][1])],
            out_send.at[which, j, r], out_recv.at[which, j, r], (g, dd),
        )

    own_copies = [
        pltpu.make_async_copy(wsl, gathered.at[mine, rows_at(d), :], own.at[0]),
        pltpu.make_async_copy(act.at[:, cols_at(k)], xa.at[rows_at(d), pl.ds(plane, span)], own.at[1]),
        pltpu.make_async_copy(grad.at[:, cols_at(k)], xg.at[rows_at(d), pl.ds(plane, span)], own.at[2]),
    ]
    others, peers = range(1, m), range(1, n)
    even = lax.rem(d, 2) == 0
    order = [m // 2] + [
        r
        for i in range(1, m - m // 2)
        for r in (jnp.where(even, m // 2 + i, m // 2 - i), jnp.where(even, m // 2 - i, m // 2 + i))
    ]
    for r in order:
        w1(r, True).start()
    for r in order:
        spread_start(0, xa, act, r)
    for c in loads[1]:
        c.wait()
    flatten(grad_raw, grad)
    for which, x, field in ((0, xa, act), (1, xg, grad)):
        @pl.when(middle(k))
        def _():
            src, dst = extra_cols(k)
            c = pltpu.make_async_copy(field.at[:, src], x.at[rows_at(d), dst], own.at[3 + which])
            c.start()
            c.wait()

    for c in own_copies:
        c.start()
    for c in own_copies:
        c.wait()
    for r in others:
        w1(r, False).wait_recv()

    @pl.when(g * per < taps)
    def _():
        for r in peers:
            w2(r, True).start()

    for r in order:
        spread_sent(0, xa, act, r)
        spread_start(1, xg, grad, r)
    spread_landed(0, xa, act)
    halo_start(0, xa)

    for r in peers:
        @pl.when(lax.rem(g + n - r, n) * per < taps)
        def _():
            w2(r, False).wait_recv()

    def filters(l, backward):
        for a in range(3):
            for b in range(3):
                for c in range(3):
                    tap = 9 * a + 3 * b + c
                    block_at = gathered[26 - tap].T if backward else gathered[tap]
                    l[pl.ds(b * chans, chans), pl.ds((3 * c + a) * chans, chans)] = block_at

    filters(lf, False)

    lane = lax.broadcasted_iota(jnp.int32, (chans, height), 1)

    def pair_sum(x, l, y, pair):
        def cells(slot, z):
            return x[:, pl.ds(slot * plane + z * height, height)]

        for z in range(depth):
            inside = [c for c in range(3) if 0 <= z + c - 1 < depth]
            right = jnp.concatenate(
                [
                    jnp.concatenate([cells(s + a - 1, z + c - 1) for s in pair], axis=1)
                    for c in inside
                    for a in range(3)
                ],
                axis=0,
            )
            left = l[:, pl.ds(inside[0] * 3 * chans, len(inside) * 3 * chans)]
            acc = jnp.dot(left, right, preferred_element_type=jnp.float32)
            for i, s in enumerate(pair):
                part = acc[:, i * height : (i + 1) * height]
                below = pltpu.roll(part[:chans], 1, 1)
                above = pltpu.roll(part[2 * chans :], height - 1, 1)
                total = (
                    part[chans : 2 * chans]
                    + jnp.where(lane > 0, below, 0.0)
                    + jnp.where(lane < height - 1, above, 0.0)
                )
                y[:, pl.ds((s - 1) * plane + z * height, height)] = total.astype(y.dtype)

    def finish(which, x, l, y, out):
        for s in range(2, block, 2):
            pair_sum(x, l, y, (s, s + 1))
        if block > 2:
            for r in order:
                collect(which, y, out, 2, r, True).start()
        halo_landed(which, x)
        pair_sum(x, l, y, (1, block))
        for r in order:
            for j in range(2):
                collect(which, y, out, j, r, True).start()
        copy = pltpu.make_async_copy(y.at[rows_at(d), :], out.at[:, cols_at(k)], own.at[3 + which])
        copy.start()
        return copy

    first_own = finish(0, xa, lf, yf, outf)
    filters(lb, True)
    spread_landed(1, xg, grad)
    halo_start(1, xg)
    second_own = finish(1, xg, lb, yg, outg)

    def unflatten(which, y, out, staged, result, own_copy):
        own_copy.wait()
        for r in others:
            for j in range(len(pieces)):
                collect(which, y, out, j, r, False).wait_recv()
        for p in range(block * m):
            staged[:, p] = out[:, pl.ds(p * plane, plane)].reshape(rows, depth, height)
        copies = [
            pltpu.make_async_copy(
                staged.at[pl.ds(i * cut, cut)], result.at[pl.ds(i * cut, cut)], loaded.at[which, i]
            )
            for i in range(8)
        ]
        for c in copies:
            c.start()
        return copies

    stores = unflatten(0, yf, outf, act_raw, out_features, first_own)
    stores += unflatten(1, yg, outg, grad_raw, out_gradient, second_own)
    for r in others:
        w1(r, True).wait_send()
        spread_sent(1, xg, grad, r)
        for which, y, out in ((0, yf, outf), (1, yg, outg)):
            for j in range(len(pieces)):
                collect(which, y, out, j, r, True).wait_send()
    halo_sent(0, xa)
    halo_sent(1, xg)
    for c in stores:
        c.wait()

    @pl.when(g * per < taps)
    def _():
        for r in peers:
            w2(r, True).wait_send()


def store(cut, features, gradient, out_features, out_gradient, sems):
    copies = [
        pltpu.make_async_copy(
            src.at[pl.ds(i * cut, cut)], dst.at[pl.ds(i * cut, cut)], sems.at[which, i]
        )
        for i in range(8)
        for which, (src, dst) in enumerate(((features, out_features), (gradient, out_gradient)))
    ]
    for c in copies:
        c.start()
    for c in copies:
        c.wait()


def local_kernel(activations, conv_weight, out_grad):
    n, m = lax.axis_size("gx"), lax.axis_size("ch")
    rows, planes, depth, height = activations.shape
    taps, chans, _ = conv_weight.shape
    block = planes // m
    plane = depth * height
    per = -(-taps // n)
    whole = jax.ShapeDtypeStruct(activations.shape, jnp.bfloat16)
    flat = pltpu.VMEM((rows, planes * plane), jnp.bfloat16)
    raw = pltpu.VMEM(activations.shape, jnp.bfloat16)
    sem = pltpu.SemaphoreType.DMA
    flops = 2 * 2 * taps * chans * chans * block * plane
    features, gradient = pl.pallas_call(
        functools.partial(kernel, (n, m, rows, block, depth, height, taps)),
        out_shape=(whole, whole),
        in_specs=[pl.BlockSpec(memory_space=pl.ANY)] * 3,
        out_specs=(pl.BlockSpec(memory_space=pl.ANY),) * 2,
        scratch_shapes=[
            raw,
            raw,
            flat,
            flat,
            pltpu.VMEM((per, rows, chans), jnp.bfloat16),
            flat,
            flat,
            pltpu.VMEM((chans, (block + 2) * plane), jnp.bfloat16),
            pltpu.VMEM((chans, (block + 2) * plane), jnp.bfloat16),
            pltpu.VMEM((per * n, chans, chans), jnp.bfloat16),
            pltpu.VMEM((3 * chans, 9 * chans), jnp.bfloat16),
            pltpu.VMEM((3 * chans, 9 * chans), jnp.bfloat16),
            pltpu.VMEM((chans, block * plane), jnp.bfloat16),
            pltpu.VMEM((chans, block * plane), jnp.bfloat16),
            sem((m,)), sem((m,)), sem((n,)), sem((n,)),
            sem((2, m)), sem((2, m)), sem((2, 2)), sem((2, 2)),
            sem((2, 3, m)), sem((2, 3, m)), sem((2, m)), sem((2, m)), sem((5,)), sem((per,)), sem((2, 8)),
        ],
        compiler_params=pltpu.CompilerParams(
            collective_id=0, has_side_effects=True, vmem_limit_bytes=60 * 2**20
        ),
        cost_estimate=pl.CostEstimate(
            flops=flops, bytes_accessed=8 * rows * planes * plane, transcendentals=0
        ),
    )(activations, out_grad, jnp.swapaxes(conv_weight, 1, 2))
    hbm = pl.BlockSpec(memory_space=pl.ANY)
    return pl.pallas_call(
        functools.partial(store, rows // 8),
        out_shape=(whole, whole),
        in_specs=[hbm] * 2,
        out_specs=(hbm, hbm),
        scratch_shapes=[sem((2, 8))],
        compiler_params=pltpu.CompilerParams(vmem_limit_bytes=60 * 2**20),
    )(features, gradient)


def local(activations, conv_weight, out_grad):
    n, m = lax.axis_size("gx"), lax.axis_size("ch")
    rows, planes, _, height = activations.shape
    fits = rows % 16 == 0 and planes % (2 * m) == 0 and height % 128 == 0 and n % 2 == 0 and m % 2 == 0
    plan = local_kernel if fits else local_plain
    return plan(activations, conv_weight, out_grad)


def solution(mesh):
    return jax.shard_map(
        local,
        mesh=mesh,
        in_specs=(P("ch", "gx", None, None), P(None, None, "ch"), P("ch", "gx", None, None)),
        out_specs=(P("ch", "gx", None, None), P("ch", "gx", None, None)),
        check_vma=False,
    )
```

```python
import functools

import jax
import jax.numpy as jnp
from jax import lax
from jax.experimental import pallas as pl
from jax.experimental.pallas import tpu as pltpu
from jax.sharding import PartitionSpec as P

MESH = pl.DeviceIdType.MESH


def with_halo(cells, sides, width):
    for axis, dim in sides:
        count = lax.axis_size(axis)
        head = lax.slice_in_dim(cells, 0, width, axis=dim)
        tail = lax.slice_in_dim(cells, cells.shape[dim] - width, cells.shape[dim], axis=dim)
        cells = jnp.concatenate(
            [
                lax.ppermute(tail, axis, [(i, (i + 1) % count) for i in range(count)]),
                cells,
                lax.ppermute(head, axis, [((i + 1) % count, i) for i in range(count)]),
            ],
            axis=dim,
        )
    return cells


def tap_sum(extended, weight, direction, pattern):
    planes = extended.shape[1] - 2
    depth = extended.shape[2]
    height = extended.shape[3]
    padded = jnp.pad(extended, ((0, 0), (0, 0), (1, 1), (1, 1)))
    summed = None
    for first in range(3):
        for second in range(3):
            for third in range(3):
                offset_x = 1 + direction * (first - 1)
                offset_y = 1 + direction * (second - 1)
                offset_z = 1 + direction * (third - 1)
                window_part = padded[
                    :,
                    offset_x : offset_x + planes,
                    offset_z : offset_z + depth,
                    offset_y : offset_y + height,
                ]
                product = jnp.einsum(
                    pattern,
                    window_part,
                    weight[9 * first + 3 * second + third],
                    preferred_element_type=jnp.float32,
                )
                summed = product if summed is None else summed + product
    return summed


def cell_faces(field):
    return with_halo(field, ((("gx", "ch"), 1),), 1)


def local_plain(activations, conv_weight, out_grad):
    full_weight = lax.all_gather(conv_weight, "ch", axis=2, tiled=True)
    cells_act, cells_grad = (
        lax.all_to_all(activations, "ch", split_axis=1, concat_axis=0, tiled=True),
        lax.all_to_all(out_grad, "ch", split_axis=1, concat_axis=0, tiled=True),
    )
    forward = tap_sum(cell_faces(cells_act), full_weight, 1, "kxzy,kn->nxzy").astype(jnp.bfloat16)
    backward = tap_sum(cell_faces(cells_grad), full_weight, -1, "kxzy,nk->nxzy").astype(
        jnp.bfloat16
    )
    return (
        lax.all_to_all(forward, "ch", split_axis=0, concat_axis=1, tiled=True),
        lax.all_to_all(backward, "ch", split_axis=0, concat_axis=1, tiled=True),
    )


def kernel(
    dims, act, grad, weight, outf, outg,
    wsl, xa, xg, gathered, lf, lb, yf, yg,
    w1_send, w1_recv, w2_send, w2_recv, in_send, in_recv, halo_send, halo_recv,
    out_send, out_recv, extra_send, extra_recv, own,
):
    n, m, rows, block, depth, height, taps = dims
    chans = m * rows
    per = -(-taps // n)
    plane = depth * height
    span = block * plane
    g = lax.axis_index("gx")
    d = lax.axis_index("ch")
    pair, c = lax.div(g, 2), lax.rem(g, 2)

    def level(pp, at):
        return jnp.where(lax.rem(pp, 2) == 0, at, m - 1 - at)

    def device_of(index):
        pp, at = lax.div(index, 2 * m), lax.rem(index, 2 * m)
        return 2 * pp + lax.rem(at, 2), level(pp, lax.div(at, 2))

    place = 2 * level(pair, d) + c
    source, k = lax.div(place, m), lax.rem(place, m)
    holds_own = source == c
    whole = n * m
    spot = pair * 2 * m + place
    prev = device_of(lax.rem(spot + whole - 1, whole))
    following = device_of(lax.rem(spot + 1, whole))

    def worker(q):
        return device_of(pair * 2 * m + c * m + q)

    def holder(dd):
        return 2 * pair + source, dd

    def rows_at(dd):
        return pl.ds(pl.multiple_of(dd * rows, rows), rows)

    def cols_at(kk):
        return pl.ds(pl.multiple_of(kk * span, 128), span)

    barrier = pltpu.get_barrier_semaphore()
    for side in range(2):
        for r in range(m):
            if side + r > 0:
                pl.semaphore_signal(
                    barrier, inc=1, device_id_type=MESH,
                    device_id=(2 * pair + lax.rem(c + side, 2), lax.rem(d + r, m)),
                )
    for r in range(2, n):
        pl.semaphore_signal(
            barrier, inc=1, device_id=(lax.rem(2 * pair + r, n), d), device_id_type=MESH
        )
    pl.semaphore_wait(barrier, 2 * m - 1 + n - 2)

    def remote(src, dst, send, recv, where):
        return pltpu.make_async_remote_copy(
            src_ref=src, dst_ref=dst, send_sem=send, recv_sem=recv,
            device_id=where, device_id_type=MESH,
        )

    mine = pl.ds(g * per, per)

    def w1(r, sending):
        dd = lax.rem(d + r, m) if sending else lax.rem(d + m - r, m)
        at = d if sending else dd
        return remote(wsl, gathered.at[mine, rows_at(at), :], w1_send.at[r], w1_recv.at[r], (g, dd))

    def w2(r, sending):
        gg = lax.rem(g + r, n) if sending else lax.rem(g + n - r, n)
        at = g if sending else gg
        part = gathered.at[pl.ds(at * per, per), :, :]
        return remote(part, part, w2_send.at[r], w2_recv.at[r], (gg, d))

    inner = pl.ds(plane, span)

    def spread_out(which, x, field, q):
        return remote(
            field.at[:, cols_at(q)], x.at[rows_at(d), inner],
            in_send.at[which, q], in_recv.at[which, d], worker(q),
        )

    def spread_in(which, x, field, dd):
        return remote(
            field.at[:, cols_at(k)], x.at[rows_at(dd), inner],
            in_send.at[which, k], in_recv.at[which, dd], holder(dd),
        )

    def foreign_work(q):
        return c * m + q != place

    def foreign_holder(dd):
        return jnp.logical_or(jnp.logical_not(holds_own), dd != d)

    low_end, high_end = pl.ds(0, plane), pl.ds(m * span - plane, plane)
    low_slot, high_slot = pl.ds(0, plane), pl.ds(span + plane, plane)
    edges = ((high_end, low_slot, m), (low_end, high_slot, m - 1))

    def extra(which, x, field, side, dd, where):
        src, dst, _ = edges[side]
        return remote(
            field.at[:, src], x.at[rows_at(dd), dst],
            extra_send.at[which], extra_recv.at[which, dd], where,
        )

    def extra_each(which, x, field, act_on):
        for side in range(2):
            @pl.when(jnp.logical_and(c == side, place != edges[side][2]))
            def _():
                act_on(extra(which, x, field, side, d, device_of(pair * 2 * m + edges[side][2])))

    def extra_landed(which, x, field):
        for side in range(2):
            @pl.when(place == edges[side][2])
            def _():
                for r in range(1, m):
                    dd = lax.rem(d + r, m)
                    extra(which, x, field, side, dd, (g, dd)).wait_recv()

    def spread_start(which, x, field, q):
        @pl.when(foreign_work(q))
        def _():
            spread_out(which, x, field, q).start()

    def spread_sent(which, x, field, q):
        @pl.when(foreign_work(q))
        def _():
            spread_out(which, x, field, q).wait_send()

    def spread_landed(which, x, field):
        for dd in range(m):
            @pl.when(foreign_holder(dd))
            def _():
                spread_in(which, x, field, dd).wait_recv()
        extra_landed(which, x, field)

    def spread_own(which, x, field):
        def move(src, dst):
            copy = pltpu.make_async_copy(field.at[:, src], x.at[rows_at(d), dst], own.at[1 + which])
            copy.start()
            copy.wait()

        @pl.when(holds_own)
        def _():
            move(cols_at(k), inner)

        for side in range(2):
            @pl.when(place == edges[side][2])
            def _():
                move(edges[side][0], edges[side][1])

    def halo(which, x, side):
        first, last = pl.ds(plane, plane), pl.ds(span, plane)
        low, high = pl.ds(0, plane), pl.ds(span + plane, plane)
        src, dst, where = ((first, high, prev), (last, low, following))[side]
        return remote(
            x.at[:, src], x.at[:, dst], halo_send.at[which, side], halo_recv.at[which, side], where
        )

    has_prev, has_next = place != m, place != m - 1
    sends, lands = (has_prev, has_next), (has_next, has_prev)

    def halo_start(which, x):
        for side in range(2):
            @pl.when(sends[side])
            def _():
                halo(which, x, side).start()

    def halo_sent(which, x):
        for side in range(2):
            @pl.when(sends[side])
            def _():
                halo(which, x, side).wait_send()

    def halo_landed(which, x):
        for side in range(2):
            @pl.when(lands[side])
            def _():
                halo(which, x, side).wait_recv()

    pieces = [(0, plane), ((block - 1) * plane, plane)]
    if block > 2:
        pieces.append((plane, (block - 2) * plane))

    def collect_out(which, y, out, j, dd):
        at, size = pieces[j]
        return remote(
            y.at[rows_at(dd), pl.ds(at, size)],
            out.at[:, pl.ds(pl.multiple_of(k * span + at, 128), size)],
            out_send.at[which, j, dd], out_recv.at[which, j, k], holder(dd),
        )

    def collect_in(which, y, out, j, q):
        at, size = pieces[j]
        return remote(
            y.at[rows_at(d), pl.ds(at, size)], out.at[:, pl.ds(q * span + at, size)],
            out_send.at[which, j, d], out_recv.at[which, j, q], worker(q),
        )

    def collect_own(which, y, out):
        return pltpu.make_async_copy(y.at[rows_at(d), :], out.at[:, cols_at(k)], own.at[3 + which])

    def collect_start(which, y, out, parts):
        for r in range(m):
            dd = lax.rem(d + r, m)

            @pl.when(foreign_holder(dd))
            def _():
                for j in parts:
                    collect_out(which, y, out, j, dd).start()

    def collect_finish(which, y, out):
        @pl.when(holds_own)
        def _():
            collect_own(which, y, out).wait()

        for q in range(m):
            @pl.when(foreign_work(q))
            def _():
                for j in range(len(pieces)):
                    collect_in(which, y, out, j, q).wait_recv()

            @pl.when(foreign_holder(q))
            def _():
                for j in range(len(pieces)):
                    collect_out(which, y, out, j, q).wait_send()

    for i in range(per):
        wsl[i] = weight[jnp.minimum(g * per + i, taps - 1)]
    others, peers = range(1, m), range(1, n)
    order = [lax.rem(d + r, m) for r in range(m)]
    for r in others:
        w1(r, True).start()
    for q in order:
        spread_start(0, xa, act, q)
    extra_each(0, xa, act, lambda copy: copy.start())
    own_filters = pltpu.make_async_copy(wsl, gathered.at[mine, rows_at(d), :], own.at[0])
    own_filters.start()
    spread_own(0, xa, act)
    spread_own(1, xg, grad)
    own_filters.wait()
    for r in others:
        w1(r, False).wait_recv()

    @pl.when(g * per < taps)
    def _():
        for r in peers:
            w2(r, True).start()

    for q in order:
        spread_sent(0, xa, act, q)
        spread_start(1, xg, grad, q)
    extra_each(1, xg, grad, lambda copy: copy.start())
    spread_landed(0, xa, act)
    halo_start(0, xa)

    for r in peers:
        @pl.when(lax.rem(g + n - r, n) * per < taps)
        def _():
            w2(r, False).wait_recv()

    def filters(l, backward):
        for a in range(3):
            for b in range(3):
                for e in range(3):
                    tap = 9 * a + 3 * b + e
                    part = gathered[taps - 1 - tap].T if backward else gathered[tap]
                    l[pl.ds(b * chans, chans), pl.ds((3 * e + a) * chans, chans)] = part

    filters(lf, False)
    lane = lax.broadcasted_iota(jnp.int32, (chans, height), 1)

    def pair_sum(x, l, y, pair):
        def cells(slot, z):
            return x[:, pl.ds(slot * plane + z * height, height)]

        for z in range(depth):
            inside = [c for c in range(3) if 0 <= z + c - 1 < depth]
            right = jnp.concatenate(
                [
                    jnp.concatenate([cells(s + a - 1, z + c - 1) for s in pair], axis=1)
                    for c in inside
                    for a in range(3)
                ],
                axis=0,
            )
            left = l[:, pl.ds(inside[0] * 3 * chans, len(inside) * 3 * chans)]
            acc = jnp.dot(left, right, preferred_element_type=jnp.float32)
            for i, s in enumerate(pair):
                part = acc[:, i * height : (i + 1) * height]
                below = pltpu.roll(part[:chans], 1, 1)
                above = pltpu.roll(part[2 * chans :], height - 1, 1)
                total = (
                    part[chans : 2 * chans]
                    + jnp.where(lane > 0, below, 0.0)
                    + jnp.where(lane < height - 1, above, 0.0)
                )
                y[:, pl.ds((s - 1) * plane + z * height, height)] = total.astype(y.dtype)

    def finish(which, x, l, y, out):
        for s in range(2, block, 2):
            pair_sum(x, l, y, (s, s + 1))
        if block > 2:
            collect_start(which, y, out, (2,))
        halo_landed(which, x)
        pair_sum(x, l, y, (1, block))
        collect_start(which, y, out, (0, 1))

        @pl.when(holds_own)
        def _():
            collect_own(which, y, out).start()

    finish(0, xa, lf, yf, outf)
    filters(lb, True)
    spread_landed(1, xg, grad)
    halo_start(1, xg)
    finish(1, xg, lb, yg, outg)

    for r in others:
        w1(r, True).wait_send()
    for q in order:
        spread_sent(1, xg, grad, q)
    for which, x, field in ((0, xa, act), (1, xg, grad)):
        extra_each(which, x, field, lambda copy: copy.wait_send())
        halo_sent(which, x)
    collect_finish(0, yf, outf)
    collect_finish(1, yg, outg)

    @pl.when(g * per < taps)
    def _():
        for r in peers:
            w2(r, True).wait_send()


def local_kernel(activations, conv_weight, out_grad):
    n, m = lax.axis_size("gx"), lax.axis_size("ch")
    rows, planes, depth, height = activations.shape
    taps, chans, _ = conv_weight.shape
    block = planes // m
    plane = depth * height
    per = -(-taps // n)
    vmem = pl.BlockSpec(memory_space=pltpu.VMEM)
    flat = jax.ShapeDtypeStruct((rows, planes * plane), jnp.bfloat16)
    sem = pltpu.SemaphoreType.DMA
    flops = 2 * 2 * taps * chans * chans * block * plane
    features, gradient = pl.pallas_call(
        functools.partial(kernel, (n, m, rows, block, depth, height, taps)),
        out_shape=(flat, flat),
        in_specs=[vmem] * 3,
        out_specs=(vmem, vmem),
        scratch_shapes=[
            pltpu.VMEM((per, rows, chans), jnp.bfloat16),
            pltpu.VMEM((chans, (block + 2) * plane), jnp.bfloat16),
            pltpu.VMEM((chans, (block + 2) * plane), jnp.bfloat16),
            pltpu.VMEM((per * n, chans, chans), jnp.bfloat16),
            pltpu.VMEM((3 * chans, 9 * chans), jnp.bfloat16),
            pltpu.VMEM((3 * chans, 9 * chans), jnp.bfloat16),
            pltpu.VMEM((chans, block * plane), jnp.bfloat16),
            pltpu.VMEM((chans, block * plane), jnp.bfloat16),
            sem((m,)), sem((m,)), sem((n,)), sem((n,)),
            sem((2, m)), sem((2, m)), sem((2, 2)), sem((2, 2)),
            sem((2, 3, m)), sem((2, 3, m)), sem((2,)), sem((2, m)), sem((5,)),
        ],
        compiler_params=pltpu.CompilerParams(
            collective_id=0, has_side_effects=True, vmem_limit_bytes=20 * 2**20
        ),
        cost_estimate=pl.CostEstimate(
            flops=flops, bytes_accessed=8 * rows * planes * plane, transcendentals=0
        ),
    )(activations.reshape(rows, -1), out_grad.reshape(rows, -1), jnp.swapaxes(conv_weight, 1, 2))
    return features.reshape(activations.shape), gradient.reshape(out_grad.shape)


def local(activations, conv_weight, out_grad):
    n, m = lax.axis_size("gx"), lax.axis_size("ch")
    rows, planes, _, height = activations.shape
    fits = rows % 16 == 0 and planes % (2 * m) == 0 and height % 128 == 0 and n % 4 == 0 and m % 2 == 0
    plan = local_kernel if fits else local_plain
    return plan(activations, conv_weight, out_grad)


def solution(mesh):
    return jax.shard_map(
        local,
        mesh=mesh,
        in_specs=(P("ch", "gx", None, None), P(None, None, "ch"), P("ch", "gx", None, None)),
        out_specs=(P("ch", "gx", None, None), P("ch", "gx", None, None)),
        check_vma=False,
    )
```

```python
import functools

import jax
import jax.numpy as jnp
from jax import lax
from jax.experimental import pallas as pl
from jax.experimental.pallas import tpu as pltpu
from jax.sharding import PartitionSpec as P

MESH = pl.DeviceIdType.MESH


def with_halo(cells, sides, width):
    for axis, dim in sides:
        count = lax.axis_size(axis)
        head = lax.slice_in_dim(cells, 0, width, axis=dim)
        tail = lax.slice_in_dim(cells, cells.shape[dim] - width, cells.shape[dim], axis=dim)
        cells = jnp.concatenate(
            [
                lax.ppermute(tail, axis, [(i, (i + 1) % count) for i in range(count)]),
                cells,
                lax.ppermute(head, axis, [((i + 1) % count, i) for i in range(count)]),
            ],
            axis=dim,
        )
    return cells


def tap_sum(extended, weight, direction, pattern):
    planes = extended.shape[1] - 2
    depth = extended.shape[2]
    height = extended.shape[3]
    padded = jnp.pad(extended, ((0, 0), (0, 0), (1, 1), (1, 1)))
    summed = None
    for first in range(3):
        for second in range(3):
            for third in range(3):
                offset_x = 1 + direction * (first - 1)
                offset_y = 1 + direction * (second - 1)
                offset_z = 1 + direction * (third - 1)
                window_part = padded[
                    :,
                    offset_x : offset_x + planes,
                    offset_z : offset_z + depth,
                    offset_y : offset_y + height,
                ]
                product = jnp.einsum(
                    pattern,
                    window_part,
                    weight[9 * first + 3 * second + third],
                    preferred_element_type=jnp.float32,
                )
                summed = product if summed is None else summed + product
    return summed


def cell_faces(field):
    return with_halo(field, ((("gx", "ch"), 1),), 1)


def local_plain(activations, conv_weight, out_grad):
    full_weight = lax.all_gather(conv_weight, "ch", axis=2, tiled=True)
    cells_act, cells_grad = (
        lax.all_to_all(activations, "ch", split_axis=1, concat_axis=0, tiled=True),
        lax.all_to_all(out_grad, "ch", split_axis=1, concat_axis=0, tiled=True),
    )
    forward = tap_sum(cell_faces(cells_act), full_weight, 1, "kxzy,kn->nxzy").astype(jnp.bfloat16)
    backward = tap_sum(cell_faces(cells_grad), full_weight, -1, "kxzy,nk->nxzy").astype(
        jnp.bfloat16
    )
    return (
        lax.all_to_all(forward, "ch", split_axis=0, concat_axis=1, tiled=True),
        lax.all_to_all(backward, "ch", split_axis=0, concat_axis=1, tiled=True),
    )


def kernel(
    dims, act, grad, weight, outf, outg,
    wsl, xa, xg, gathered, lf, lb, yf, yg,
    w1_send, w1_recv, w2_send, w2_recv, in_send, in_recv, halo_send, halo_recv,
    out_send, out_recv, extra_send, extra_recv, own,
):
    n, m, rows, block, depth, height, taps = dims
    chans = m * rows
    per = -(-taps // n)
    plane = depth * height
    span = block * plane
    g = lax.axis_index("gx")
    d = lax.axis_index("ch")
    pair, c = lax.div(g, 2), lax.rem(g, 2)

    def level(pp, at):
        return jnp.where(lax.rem(pp, 2) == 0, at, m - 1 - at)

    def device_of(index):
        pp, at = lax.div(index, 2 * m), lax.rem(index, 2 * m)
        return 2 * pp + lax.rem(at, 2), level(pp, lax.div(at, 2))

    place = 2 * level(pair, d) + c
    source, k = lax.div(place, m), lax.rem(place, m)
    holds_own = source == c
    whole = n * m
    spot = pair * 2 * m + place
    prev = device_of(lax.rem(spot + whole - 1, whole))
    following = device_of(lax.rem(spot + 1, whole))

    def worker(q):
        return device_of(pair * 2 * m + c * m + q)

    def holder(dd):
        return 2 * pair + source, dd

    def rows_at(dd):
        return pl.ds(pl.multiple_of(dd * rows, rows), rows)

    def cols_at(kk):
        return pl.ds(pl.multiple_of(kk * span, 128), span)

    barrier = pltpu.get_barrier_semaphore()
    for side in range(2):
        for r in range(m):
            if side + r > 0:
                pl.semaphore_signal(
                    barrier, inc=1, device_id_type=MESH,
                    device_id=(2 * pair + lax.rem(c + side, 2), lax.rem(d + r, m)),
                )
    for r in range(2, n):
        pl.semaphore_signal(
            barrier, inc=1, device_id=(lax.rem(2 * pair + r, n), d), device_id_type=MESH
        )
    pl.semaphore_wait(barrier, 2 * m - 1 + n - 2)

    def remote(src, dst, send, recv, where):
        return pltpu.make_async_remote_copy(
            src_ref=src, dst_ref=dst, send_sem=send, recv_sem=recv,
            device_id=where, device_id_type=MESH,
        )

    mine = pl.ds(g * per, per)

    half = m // 2
    across = lax.rem(d + half, m)
    base = lax.div(d, half) * half

    def w1(sending):
        at = rows_at(d if sending else across)
        return remote(wsl, gathered.at[mine, at, :], w1_send.at[0], w1_recv.at[0], (g, across))

    def w1_share(r, far, sending):
        dd = base + lax.rem(d - base + (r if sending else half - r), half)
        at = d if sending else dd
        part = gathered.at[mine, rows_at(lax.rem(at + half, m) if far else at), :]
        slot = 1 + 2 * (r - 1) + far
        return remote(part, part, w1_send.at[slot], w1_recv.at[slot], (g, dd))

    shares = [(r, far) for r in range(1, half) for far in range(2)]

    def w2(r, sending):
        gg = lax.rem(g + r, n) if sending else lax.rem(g + n - r, n)
        at = g if sending else gg
        part = gathered.at[pl.ds(at * per, per), :, :]
        return remote(part, part, w2_send.at[r], w2_recv.at[r], (gg, d))

    inner = pl.ds(plane, span)

    def spread_out(which, x, field, q):
        return remote(
            field.at[:, cols_at(q)], x.at[rows_at(d), inner],
            in_send.at[which, q], in_recv.at[which, d], worker(q),
        )

    def spread_in(which, x, field, dd):
        return remote(
            field.at[:, cols_at(k)], x.at[rows_at(dd), inner],
            in_send.at[which, k], in_recv.at[which, dd], holder(dd),
        )

    def foreign_work(q):
        return c * m + q != place

    def foreign_holder(dd):
        return jnp.logical_or(jnp.logical_not(holds_own), dd != d)

    low_end, high_end = pl.ds(0, plane), pl.ds(m * span - plane, plane)
    low_slot, high_slot = pl.ds(0, plane), pl.ds(span + plane, plane)
    edges = ((high_end, low_slot, m), (low_end, high_slot, m - 1))

    def extra(which, x, field, side, dd, where):
        src, dst, _ = edges[side]
        return remote(
            field.at[:, src], x.at[rows_at(dd), dst],
            extra_send.at[which], extra_recv.at[which, dd], where,
        )

    def extra_each(which, x, field, act_on):
        for side in range(2):
            @pl.when(jnp.logical_and(c == side, place != edges[side][2]))
            def _():
                act_on(extra(which, x, field, side, d, device_of(pair * 2 * m + edges[side][2])))

    def extra_landed(which, x, field):
        for side in range(2):
            @pl.when(place == edges[side][2])
            def _():
                for r in range(1, m):
                    dd = lax.rem(d + r, m)
                    extra(which, x, field, side, dd, (g, dd)).wait_recv()

    def spread_start(which, x, field, q):
        @pl.when(foreign_work(q))
        def _():
            spread_out(which, x, field, q).start()

    def spread_sent(which, x, field, q):
        @pl.when(foreign_work(q))
        def _():
            spread_out(which, x, field, q).wait_send()

    def spread_landed(which, x, field):
        for dd in range(m):
            @pl.when(foreign_holder(dd))
            def _():
                spread_in(which, x, field, dd).wait_recv()
        extra_landed(which, x, field)

    def spread_own(which, x, field):
        def move(src, dst):
            copy = pltpu.make_async_copy(field.at[:, src], x.at[rows_at(d), dst], own.at[1 + which])
            copy.start()
            copy.wait()

        @pl.when(holds_own)
        def _():
            move(cols_at(k), inner)

        for side in range(2):
            @pl.when(place == edges[side][2])
            def _():
                move(edges[side][0], edges[side][1])

    def halo(which, x, side):
        first, last = pl.ds(plane, plane), pl.ds(span, plane)
        low, high = pl.ds(0, plane), pl.ds(span + plane, plane)
        src, dst, where = ((first, high, prev), (last, low, following))[side]
        return remote(
            x.at[:, src], x.at[:, dst], halo_send.at[which, side], halo_recv.at[which, side], where
        )

    has_prev, has_next = place != m, place != m - 1
    sends, lands = (has_prev, has_next), (has_next, has_prev)

    def halo_start(which, x):
        for side in range(2):
            @pl.when(sends[side])
            def _():
                halo(which, x, side).start()

    def halo_sent(which, x):
        for side in range(2):
            @pl.when(sends[side])
            def _():
                halo(which, x, side).wait_send()

    def halo_landed(which, x):
        for side in range(2):
            @pl.when(lands[side])
            def _():
                halo(which, x, side).wait_recv()

    pieces = [(0, plane), ((block - 1) * plane, plane)]
    if block > 2:
        pieces.append((plane, (block - 2) * plane))

    def collect_out(which, y, out, j, dd):
        at, size = pieces[j]
        return remote(
            y.at[rows_at(dd), pl.ds(at, size)],
            out.at[:, pl.ds(pl.multiple_of(k * span + at, 128), size)],
            out_send.at[which, j, dd], out_recv.at[which, j, k], holder(dd),
        )

    def collect_in(which, y, out, j, q):
        at, size = pieces[j]
        return remote(
            y.at[rows_at(d), pl.ds(at, size)], out.at[:, pl.ds(q * span + at, size)],
            out_send.at[which, j, d], out_recv.at[which, j, q], worker(q),
        )

    def collect_own(which, y, out):
        return pltpu.make_async_copy(y.at[rows_at(d), :], out.at[:, cols_at(k)], own.at[3 + which])

    def collect_start(which, y, out, parts):
        for r in range(m):
            dd = lax.rem(d + r, m)

            @pl.when(foreign_holder(dd))
            def _():
                for j in parts:
                    collect_out(which, y, out, j, dd).start()

    def collect_finish(which, y, out):
        @pl.when(holds_own)
        def _():
            collect_own(which, y, out).wait()

        for q in range(m):
            @pl.when(foreign_work(q))
            def _():
                for j in range(len(pieces)):
                    collect_in(which, y, out, j, q).wait_recv()

            @pl.when(foreign_holder(q))
            def _():
                for j in range(len(pieces)):
                    collect_out(which, y, out, j, q).wait_send()

    for i in range(per):
        wsl[i] = weight[jnp.minimum(g * per + i, taps - 1)]
    peers = range(1, n)
    order = [lax.rem(d + r, m) for r in range(m)]
    w1(True).start()
    for q in order:
        spread_start(0, xa, act, q)
    extra_each(0, xa, act, lambda copy: copy.start())
    own_filters = pltpu.make_async_copy(wsl, gathered.at[mine, rows_at(d), :], own.at[0])
    own_filters.start()
    own_filters.wait()
    for r in range(1, half):
        w1_share(r, 0, True).start()
    spread_own(0, xa, act)
    spread_own(1, xg, grad)
    w1(False).wait_recv()
    for r in range(1, half):
        w1_share(r, 1, True).start()
    for r, far in shares:
        w1_share(r, far, False).wait_recv()

    @pl.when(g * per < taps)
    def _():
        for r in peers:
            w2(r, True).start()

    for q in order:
        spread_sent(0, xa, act, q)
        spread_start(1, xg, grad, q)
    extra_each(1, xg, grad, lambda copy: copy.start())
    spread_landed(0, xa, act)
    halo_start(0, xa)

    for r in peers:
        @pl.when(lax.rem(g + n - r, n) * per < taps)
        def _():
            w2(r, False).wait_recv()

    def filters(l, backward):
        for a in range(3):
            for b in range(3):
                for e in range(3):
                    tap = 9 * a + 3 * b + e
                    part = gathered[taps - 1 - tap].T if backward else gathered[tap]
                    l[pl.ds(b * chans, chans), pl.ds((3 * e + a) * chans, chans)] = part

    filters(lf, False)
    lane = lax.broadcasted_iota(jnp.int32, (chans, height), 1)

    def pair_sum(x, l, y, pair):
        def cells(slot, z):
            return x[:, pl.ds(slot * plane + z * height, height)]

        for z in range(depth):
            inside = [c for c in range(3) if 0 <= z + c - 1 < depth]
            right = jnp.concatenate(
                [
                    jnp.concatenate([cells(s + a - 1, z + c - 1) for s in pair], axis=1)
                    for c in inside
                    for a in range(3)
                ],
                axis=0,
            )
            left = l[:, pl.ds(inside[0] * 3 * chans, len(inside) * 3 * chans)]
            acc = jnp.dot(left, right, preferred_element_type=jnp.float32)
            for i, s in enumerate(pair):
                part = acc[:, i * height : (i + 1) * height]
                below = pltpu.roll(part[:chans], 1, 1)
                above = pltpu.roll(part[2 * chans :], height - 1, 1)
                total = (
                    part[chans : 2 * chans]
                    + jnp.where(lane > 0, below, 0.0)
                    + jnp.where(lane < height - 1, above, 0.0)
                )
                y[:, pl.ds((s - 1) * plane + z * height, height)] = total.astype(y.dtype)

    def finish(which, x, l, y, out):
        for s in range(2, block, 2):
            pair_sum(x, l, y, (s, s + 1))
        if block > 2:
            collect_start(which, y, out, (2,))
        halo_landed(which, x)
        pair_sum(x, l, y, (1, block))
        collect_start(which, y, out, (0, 1))

        @pl.when(holds_own)
        def _():
            collect_own(which, y, out).start()

    finish(0, xa, lf, yf, outf)
    filters(lb, True)
    spread_landed(1, xg, grad)
    halo_start(1, xg)
    finish(1, xg, lb, yg, outg)

    w1(True).wait_send()
    for r, far in shares:
        w1_share(r, far, True).wait_send()
    for q in order:
        spread_sent(1, xg, grad, q)
    for which, x, field in ((0, xa, act), (1, xg, grad)):
        extra_each(which, x, field, lambda copy: copy.wait_send())
        halo_sent(which, x)
    collect_finish(0, yf, outf)
    collect_finish(1, yg, outg)

    @pl.when(g * per < taps)
    def _():
        for r in peers:
            w2(r, True).wait_send()


def local_kernel(activations, conv_weight, out_grad):
    n, m = lax.axis_size("gx"), lax.axis_size("ch")
    rows, planes, depth, height = activations.shape
    taps, chans, _ = conv_weight.shape
    block = planes // m
    plane = depth * height
    per = -(-taps // n)
    vmem = pl.BlockSpec(memory_space=pltpu.VMEM)
    flat = jax.ShapeDtypeStruct((rows, planes * plane), jnp.bfloat16)
    sem = pltpu.SemaphoreType.DMA
    flops = 2 * 2 * taps * chans * chans * block * plane
    features, gradient = pl.pallas_call(
        functools.partial(kernel, (n, m, rows, block, depth, height, taps)),
        out_shape=(flat, flat),
        in_specs=[vmem] * 3,
        out_specs=(vmem, vmem),
        scratch_shapes=[
            pltpu.VMEM((per, rows, chans), jnp.bfloat16),
            pltpu.VMEM((chans, (block + 2) * plane), jnp.bfloat16),
            pltpu.VMEM((chans, (block + 2) * plane), jnp.bfloat16),
            pltpu.VMEM((per * n, chans, chans), jnp.bfloat16),
            pltpu.VMEM((3 * chans, 9 * chans), jnp.bfloat16),
            pltpu.VMEM((3 * chans, 9 * chans), jnp.bfloat16),
            pltpu.VMEM((chans, block * plane), jnp.bfloat16),
            pltpu.VMEM((chans, block * plane), jnp.bfloat16),
            sem((m,)), sem((m,)), sem((n,)), sem((n,)),
            sem((2, m)), sem((2, m)), sem((2, 2)), sem((2, 2)),
            sem((2, 3, m)), sem((2, 3, m)), sem((2,)), sem((2, m)), sem((5,)),
        ],
        compiler_params=pltpu.CompilerParams(
            collective_id=0, has_side_effects=True, vmem_limit_bytes=20 * 2**20
        ),
        cost_estimate=pl.CostEstimate(
            flops=flops, bytes_accessed=8 * rows * planes * plane, transcendentals=0
        ),
    )(activations.reshape(rows, -1), out_grad.reshape(rows, -1), jnp.swapaxes(conv_weight, 1, 2))
    return features.reshape(activations.shape), gradient.reshape(out_grad.shape)


def local(activations, conv_weight, out_grad):
    n, m = lax.axis_size("gx"), lax.axis_size("ch")
    rows, planes, _, height = activations.shape
    fits = rows % 16 == 0 and planes % (2 * m) == 0 and height % 128 == 0 and n % 4 == 0 and m % 2 == 0
    plan = local_kernel if fits else local_plain
    return plan(activations, conv_weight, out_grad)


def solution(mesh):
    return jax.shard_map(
        local,
        mesh=mesh,
        in_specs=(P("ch", "gx", None, None), P(None, None, "ch"), P("ch", "gx", None, None)),
        out_specs=(P("ch", "gx", None, None), P("ch", "gx", None, None)),
        check_vma=False,
    )
```

```python
import functools

import jax
import jax.numpy as jnp
from jax import lax
from jax.experimental import pallas as pl
from jax.experimental.pallas import tpu as pltpu
from jax.sharding import PartitionSpec as P

MESH = pl.DeviceIdType.MESH


def with_halo(cells, sides, width):
    for axis, dim in sides:
        count = lax.axis_size(axis)
        head = lax.slice_in_dim(cells, 0, width, axis=dim)
        tail = lax.slice_in_dim(cells, cells.shape[dim] - width, cells.shape[dim], axis=dim)
        cells = jnp.concatenate(
            [
                lax.ppermute(tail, axis, [(i, (i + 1) % count) for i in range(count)]),
                cells,
                lax.ppermute(head, axis, [((i + 1) % count, i) for i in range(count)]),
            ],
            axis=dim,
        )
    return cells


def tap_sum(extended, weight, direction, pattern):
    planes = extended.shape[1] - 2
    depth = extended.shape[2]
    height = extended.shape[3]
    padded = jnp.pad(extended, ((0, 0), (0, 0), (1, 1), (1, 1)))
    summed = None
    for first in range(3):
        for second in range(3):
            for third in range(3):
                offset_x = 1 + direction * (first - 1)
                offset_y = 1 + direction * (second - 1)
                offset_z = 1 + direction * (third - 1)
                window_part = padded[
                    :,
                    offset_x : offset_x + planes,
                    offset_z : offset_z + depth,
                    offset_y : offset_y + height,
                ]
                product = jnp.einsum(
                    pattern,
                    window_part,
                    weight[9 * first + 3 * second + third],
                    preferred_element_type=jnp.float32,
                )
                summed = product if summed is None else summed + product
    return summed


def cell_faces(field):
    return with_halo(field, ((("gx", "ch"), 1),), 1)


def local_plain(activations, conv_weight, out_grad):
    full_weight = lax.all_gather(conv_weight, "ch", axis=2, tiled=True)
    cells_act, cells_grad = (
        lax.all_to_all(activations, "ch", split_axis=1, concat_axis=0, tiled=True),
        lax.all_to_all(out_grad, "ch", split_axis=1, concat_axis=0, tiled=True),
    )
    forward = tap_sum(cell_faces(cells_act), full_weight, 1, "kxzy,kn->nxzy").astype(jnp.bfloat16)
    backward = tap_sum(cell_faces(cells_grad), full_weight, -1, "kxzy,nk->nxzy").astype(
        jnp.bfloat16
    )
    return (
        lax.all_to_all(forward, "ch", split_axis=0, concat_axis=1, tiled=True),
        lax.all_to_all(backward, "ch", split_axis=0, concat_axis=1, tiled=True),
    )


def kernel(
    dims, act, grad, weight, outf, outg,
    wsl, xa, xg, gathered, lf, lb, yf, yg,
    w1_send, w1_recv, w2_send, w2_recv, in_send, in_recv, halo_send, halo_recv,
    out_send, out_recv, extra_send, extra_recv, own,
):
    n, m, rows, block, depth, height, taps = dims
    chans = m * rows
    per = -(-taps // n)
    plane = depth * height
    span = block * plane
    g = lax.axis_index("gx")
    d = lax.axis_index("ch")
    pair, c = lax.div(g, 2), lax.rem(g, 2)

    def level(pp, at):
        return jnp.where(lax.rem(pp, 2) == 0, at, m - 1 - at)

    def device_of(index):
        pp, at = lax.div(index, 2 * m), lax.rem(index, 2 * m)
        return 2 * pp + lax.rem(at, 2), level(pp, lax.div(at, 2))

    place = 2 * level(pair, d) + c
    source, k = lax.div(place, m), lax.rem(place, m)
    holds_own = source == c
    whole = n * m
    spot = pair * 2 * m + place
    prev = device_of(lax.rem(spot + whole - 1, whole))
    following = device_of(lax.rem(spot + 1, whole))

    def worker(q):
        return device_of(pair * 2 * m + c * m + q)

    def holder(dd):
        return 2 * pair + source, dd

    def rows_at(dd):
        return pl.ds(pl.multiple_of(dd * rows, rows), rows)

    def cols_at(kk):
        return pl.ds(pl.multiple_of(kk * span, 128), span)

    barrier = pltpu.get_barrier_semaphore()
    for side in range(2):
        for r in range(m):
            if side + r > 0:
                pl.semaphore_signal(
                    barrier, inc=1, device_id_type=MESH,
                    device_id=(2 * pair + lax.rem(c + side, 2), lax.rem(d + r, m)),
                )
    for r in range(2, n):
        pl.semaphore_signal(
            barrier, inc=1, device_id=(lax.rem(2 * pair + r, n), d), device_id_type=MESH
        )
    pl.semaphore_wait(barrier, 2 * m - 1 + n - 2)

    def remote(src, dst, send, recv, where):
        return pltpu.make_async_remote_copy(
            src_ref=src, dst_ref=dst, send_sem=send, recv_sem=recv,
            device_id=where, device_id_type=MESH,
        )

    mine = pl.ds(g * per, per)

    half = m // 2
    across = lax.rem(d + half, m)
    base = lax.div(d, half) * half

    def w1(sending):
        at = rows_at(d if sending else across)
        return remote(wsl, gathered.at[mine, at, :], w1_send.at[0], w1_recv.at[0], (g, across))

    def w1_share(r, far, sending):
        dd = base + lax.rem(d - base + (r if sending else half - r), half)
        at = d if sending else dd
        part = gathered.at[mine, rows_at(lax.rem(at + half, m) if far else at), :]
        slot = 1 + 2 * (r - 1) + far
        return remote(part, part, w1_send.at[slot], w1_recv.at[slot], (g, dd))

    shares = [(r, far) for r in range(1, half) for far in range(2)]

    sibling = 2 * pair + 1 - c

    def slab(at):
        return gathered.at[pl.ds(at * per, per), :, :]

    def full(at):
        return at * per < taps

    def w2(r, sending):
        gg = lax.rem(g + r, n) if sending else lax.rem(g + n - r, n)
        part = slab(g if sending else gg)
        return remote(part, part, w2_send.at[r], w2_recv.at[r], (gg, d))

    def pass_on(r, sending):
        at = lax.rem((g if sending else sibling) + n - r, n)
        copy = remote(slab(at), slab(at), w2_send.at[r + 1], w2_recv.at[r + 1], (sibling, d))
        return full(at), copy

    inner = pl.ds(plane, span)

    def spread_out(which, x, field, q):
        return remote(
            field.at[:, cols_at(q)], x.at[rows_at(d), inner],
            in_send.at[which, q], in_recv.at[which, d], worker(q),
        )

    def spread_in(which, x, field, dd):
        return remote(
            field.at[:, cols_at(k)], x.at[rows_at(dd), inner],
            in_send.at[which, k], in_recv.at[which, dd], holder(dd),
        )

    def foreign_work(q):
        return c * m + q != place

    def foreign_holder(dd):
        return jnp.logical_or(jnp.logical_not(holds_own), dd != d)

    low_end, high_end = pl.ds(0, plane), pl.ds(m * span - plane, plane)
    low_slot, high_slot = pl.ds(0, plane), pl.ds(span + plane, plane)
    edges = ((high_end, low_slot, m), (low_end, high_slot, m - 1))

    def extra(which, x, field, side, dd, where):
        src, dst, _ = edges[side]
        return remote(
            field.at[:, src], x.at[rows_at(dd), dst],
            extra_send.at[which], extra_recv.at[which, dd], where,
        )

    def extra_each(which, x, field, act_on):
        for side in range(2):
            @pl.when(jnp.logical_and(c == side, place != edges[side][2]))
            def _():
                act_on(extra(which, x, field, side, d, device_of(pair * 2 * m + edges[side][2])))

    def extra_landed(which, x, field):
        for side in range(2):
            @pl.when(place == edges[side][2])
            def _():
                for r in range(1, m):
                    dd = lax.rem(d + r, m)
                    extra(which, x, field, side, dd, (g, dd)).wait_recv()

    def spread_start(which, x, field, q):
        @pl.when(foreign_work(q))
        def _():
            spread_out(which, x, field, q).start()

    def spread_sent(which, x, field, q):
        @pl.when(foreign_work(q))
        def _():
            spread_out(which, x, field, q).wait_send()

    def spread_landed(which, x, field):
        for dd in range(m):
            @pl.when(foreign_holder(dd))
            def _():
                spread_in(which, x, field, dd).wait_recv()
        extra_landed(which, x, field)

    def spread_own(which, x, field):
        def move(src, dst):
            copy = pltpu.make_async_copy(field.at[:, src], x.at[rows_at(d), dst], own.at[1 + which])
            copy.start()
            copy.wait()

        @pl.when(holds_own)
        def _():
            move(cols_at(k), inner)

        for side in range(2):
            @pl.when(place == edges[side][2])
            def _():
                move(edges[side][0], edges[side][1])

    def halo(which, x, side):
        first, last = pl.ds(plane, plane), pl.ds(span, plane)
        low, high = pl.ds(0, plane), pl.ds(span + plane, plane)
        src, dst, where = ((first, high, prev), (last, low, following))[side]
        return remote(
            x.at[:, src], x.at[:, dst], halo_send.at[which, side], halo_recv.at[which, side], where
        )

    has_prev, has_next = place != m, place != m - 1
    sends, lands = (has_prev, has_next), (has_next, has_prev)

    def halo_start(which, x):
        for side in range(2):
            @pl.when(sends[side])
            def _():
                halo(which, x, side).start()

    def halo_sent(which, x):
        for side in range(2):
            @pl.when(sends[side])
            def _():
                halo(which, x, side).wait_send()

    def halo_landed(which, x):
        for side in range(2):
            @pl.when(lands[side])
            def _():
                halo(which, x, side).wait_recv()

    pieces = [(0, plane), ((block - 1) * plane, plane)]
    if block > 2:
        pieces.append((plane, (block - 2) * plane))

    def collect_out(which, y, out, j, dd):
        at, size = pieces[j]
        return remote(
            y.at[rows_at(dd), pl.ds(at, size)],
            out.at[:, pl.ds(pl.multiple_of(k * span + at, 128), size)],
            out_send.at[which, j, dd], out_recv.at[which, j, k], holder(dd),
        )

    def collect_in(which, y, out, j, q):
        at, size = pieces[j]
        return remote(
            y.at[rows_at(d), pl.ds(at, size)], out.at[:, pl.ds(q * span + at, size)],
            out_send.at[which, j, d], out_recv.at[which, j, q], worker(q),
        )

    def collect_own(which, y, out):
        return pltpu.make_async_copy(y.at[rows_at(d), :], out.at[:, cols_at(k)], own.at[3 + which])

    def collect_start(which, y, out, parts):
        for r in range(m):
            dd = lax.rem(d + r, m)

            @pl.when(foreign_holder(dd))
            def _():
                for j in parts:
                    collect_out(which, y, out, j, dd).start()

    def collect_finish(which, y, out):
        @pl.when(holds_own)
        def _():
            collect_own(which, y, out).wait()

        for q in range(m):
            @pl.when(foreign_work(q))
            def _():
                for j in range(len(pieces)):
                    collect_in(which, y, out, j, q).wait_recv()

            @pl.when(foreign_holder(q))
            def _():
                for j in range(len(pieces)):
                    collect_out(which, y, out, j, q).wait_send()

    for i in range(per):
        wsl[i] = weight[jnp.minimum(g * per + i, taps - 1)]
    order = [lax.rem(d + r, m) for r in range(m)]
    w1(True).start()
    for q in order:
        spread_start(0, xa, act, q)
    extra_each(0, xa, act, lambda copy: copy.start())
    own_filters = pltpu.make_async_copy(wsl, gathered.at[mine, rows_at(d), :], own.at[0])
    own_filters.start()
    own_filters.wait()
    for r in range(1, half):
        w1_share(r, 0, True).start()
    spread_own(0, xa, act)
    spread_own(1, xg, grad)
    w1(False).wait_recv()
    for r in range(1, half):
        w1_share(r, 1, True).start()
    for r, far in shares:
        w1_share(r, far, False).wait_recv()

    steps = range(2, n, 2)

    @pl.when(full(g))
    def _():
        for r in steps:
            w2(r, True).start()
        pass_on(0, True)[1].start()

    for r in steps:
        @pl.when(full(lax.rem(g + n - r, n)))
        def _():
            w2(r, False).wait_recv()
            pass_on(r, True)[1].start()

    for q in order:
        spread_sent(0, xa, act, q)
        spread_start(1, xg, grad, q)
    extra_each(1, xg, grad, lambda copy: copy.start())
    spread_landed(0, xa, act)
    halo_start(0, xa)

    for r in range(0, n, 2):
        here, copy = pass_on(r, False)

        @pl.when(here)
        def _():
            copy.wait_recv()

    def filters(l, backward):
        for a in range(3):
            for b in range(3):
                for e in range(3):
                    tap = 9 * a + 3 * b + e
                    part = gathered[taps - 1 - tap].T if backward else gathered[tap]
                    l[pl.ds(b * chans, chans), pl.ds((3 * e + a) * chans, chans)] = part

    filters(lf, False)
    lane = lax.broadcasted_iota(jnp.int32, (chans, height), 1)

    def pair_sum(x, l, y, pair):
        def cells(slot, z):
            return x[:, pl.ds(slot * plane + z * height, height)]

        for z in range(depth):
            inside = [c for c in range(3) if 0 <= z + c - 1 < depth]
            right = jnp.concatenate(
                [
                    jnp.concatenate([cells(s + a - 1, z + c - 1) for s in pair], axis=1)
                    for c in inside
                    for a in range(3)
                ],
                axis=0,
            )
            left = l[:, pl.ds(inside[0] * 3 * chans, len(inside) * 3 * chans)]
            acc = jnp.dot(left, right, preferred_element_type=jnp.float32)
            for i, s in enumerate(pair):
                part = acc[:, i * height : (i + 1) * height]
                below = pltpu.roll(part[:chans], 1, 1)
                above = pltpu.roll(part[2 * chans :], height - 1, 1)
                total = (
                    part[chans : 2 * chans]
                    + jnp.where(lane > 0, below, 0.0)
                    + jnp.where(lane < height - 1, above, 0.0)
                )
                y[:, pl.ds((s - 1) * plane + z * height, height)] = total.astype(y.dtype)

    def finish(which, x, l, y, out):
        for s in range(2, block, 2):
            pair_sum(x, l, y, (s, s + 1))
        if block > 2:
            collect_start(which, y, out, (2,))
        halo_landed(which, x)
        pair_sum(x, l, y, (1, block))
        collect_start(which, y, out, (0, 1))

        @pl.when(holds_own)
        def _():
            collect_own(which, y, out).start()

    finish(0, xa, lf, yf, outf)
    filters(lb, True)
    spread_landed(1, xg, grad)
    halo_start(1, xg)
    finish(1, xg, lb, yg, outg)

    w1(True).wait_send()
    for r, far in shares:
        w1_share(r, far, True).wait_send()
    for q in order:
        spread_sent(1, xg, grad, q)
    for which, x, field in ((0, xa, act), (1, xg, grad)):
        extra_each(which, x, field, lambda copy: copy.wait_send())
        halo_sent(which, x)
    collect_finish(0, yf, outf)
    collect_finish(1, yg, outg)

    @pl.when(full(g))
    def _():
        for r in steps:
            w2(r, True).wait_send()

    for r in range(0, n, 2):
        here, copy = pass_on(r, True)

        @pl.when(here)
        def _():
            copy.wait_send()


def local_kernel(activations, conv_weight, out_grad):
    n, m = lax.axis_size("gx"), lax.axis_size("ch")
    rows, planes, depth, height = activations.shape
    taps, chans, _ = conv_weight.shape
    block = planes // m
    plane = depth * height
    per = -(-taps // n)
    vmem = pl.BlockSpec(memory_space=pltpu.VMEM)
    flat = jax.ShapeDtypeStruct((rows, planes * plane), jnp.bfloat16)
    sem = pltpu.SemaphoreType.DMA
    flops = 2 * 2 * taps * chans * chans * block * plane
    features, gradient = pl.pallas_call(
        functools.partial(kernel, (n, m, rows, block, depth, height, taps)),
        out_shape=(flat, flat),
        in_specs=[vmem] * 3,
        out_specs=(vmem, vmem),
        scratch_shapes=[
            pltpu.VMEM((per, rows, chans), jnp.bfloat16),
            pltpu.VMEM((chans, (block + 2) * plane), jnp.bfloat16),
            pltpu.VMEM((chans, (block + 2) * plane), jnp.bfloat16),
            pltpu.VMEM((per * n, chans, chans), jnp.bfloat16),
            pltpu.VMEM((3 * chans, 9 * chans), jnp.bfloat16),
            pltpu.VMEM((3 * chans, 9 * chans), jnp.bfloat16),
            pltpu.VMEM((chans, block * plane), jnp.bfloat16),
            pltpu.VMEM((chans, block * plane), jnp.bfloat16),
            sem((m,)), sem((m,)), sem((n,)), sem((n,)),
            sem((2, m)), sem((2, m)), sem((2, 2)), sem((2, 2)),
            sem((2, 3, m)), sem((2, 3, m)), sem((2,)), sem((2, m)), sem((5,)),
        ],
        compiler_params=pltpu.CompilerParams(
            collective_id=0, has_side_effects=True, vmem_limit_bytes=20 * 2**20
        ),
        cost_estimate=pl.CostEstimate(
            flops=flops, bytes_accessed=8 * rows * planes * plane, transcendentals=0
        ),
    )(activations.reshape(rows, -1), out_grad.reshape(rows, -1), jnp.swapaxes(conv_weight, 1, 2))
    return features.reshape(activations.shape), gradient.reshape(out_grad.shape)


def local(activations, conv_weight, out_grad):
    n, m = lax.axis_size("gx"), lax.axis_size("ch")
    rows, planes, _, height = activations.shape
    fits = rows % 16 == 0 and planes % (2 * m) == 0 and height % 128 == 0 and n % 4 == 0 and m % 2 == 0
    plan = local_kernel if fits else local_plain
    return plan(activations, conv_weight, out_grad)


def solution(mesh):
    return jax.shard_map(
        local,
        mesh=mesh,
        in_specs=(P("ch", "gx", None, None), P(None, None, "ch"), P("ch", "gx", None, None)),
        out_specs=(P("ch", "gx", None, None), P("ch", "gx", None, None)),
        check_vma=False,
    )
```

```python
import functools

import jax
import jax.numpy as jnp
from jax import lax
from jax.experimental import pallas as pl
from jax.experimental.pallas import tpu as pltpu
from jax.sharding import PartitionSpec as P

MESH = pl.DeviceIdType.MESH


def with_halo(cells, sides, width):
    for axis, dim in sides:
        count = lax.axis_size(axis)
        head = lax.slice_in_dim(cells, 0, width, axis=dim)
        tail = lax.slice_in_dim(cells, cells.shape[dim] - width, cells.shape[dim], axis=dim)
        cells = jnp.concatenate(
            [
                lax.ppermute(tail, axis, [(i, (i + 1) % count) for i in range(count)]),
                cells,
                lax.ppermute(head, axis, [((i + 1) % count, i) for i in range(count)]),
            ],
            axis=dim,
        )
    return cells


def tap_sum(extended, weight, direction, pattern):
    planes = extended.shape[1] - 2
    depth = extended.shape[2]
    height = extended.shape[3]
    padded = jnp.pad(extended, ((0, 0), (0, 0), (1, 1), (1, 1)))
    summed = None
    for first in range(3):
        for second in range(3):
            for third in range(3):
                offset_x = 1 + direction * (first - 1)
                offset_y = 1 + direction * (second - 1)
                offset_z = 1 + direction * (third - 1)
                window_part = padded[
                    :,
                    offset_x : offset_x + planes,
                    offset_z : offset_z + depth,
                    offset_y : offset_y + height,
                ]
                product = jnp.einsum(
                    pattern,
                    window_part,
                    weight[9 * first + 3 * second + third],
                    preferred_element_type=jnp.float32,
                )
                summed = product if summed is None else summed + product
    return summed


def cell_faces(field):
    return with_halo(field, ((("gx", "ch"), 1),), 1)


def local_plain(activations, conv_weight, out_grad):
    full_weight = lax.all_gather(conv_weight, "ch", axis=2, tiled=True)
    cells_act, cells_grad = (
        lax.all_to_all(activations, "ch", split_axis=1, concat_axis=0, tiled=True),
        lax.all_to_all(out_grad, "ch", split_axis=1, concat_axis=0, tiled=True),
    )
    forward = tap_sum(cell_faces(cells_act), full_weight, 1, "kxzy,kn->nxzy").astype(jnp.bfloat16)
    backward = tap_sum(cell_faces(cells_grad), full_weight, -1, "kxzy,nk->nxzy").astype(
        jnp.bfloat16
    )
    return (
        lax.all_to_all(forward, "ch", split_axis=0, concat_axis=1, tiled=True),
        lax.all_to_all(backward, "ch", split_axis=0, concat_axis=1, tiled=True),
    )


def kernel(
    dims, act, grad, weight, outf, outg,
    wsl, xa, xg, gathered, lf, lb, yf, yg,
    w1_send, w1_recv, w2_send, w2_recv, in_send, in_recv, halo_send, halo_recv,
    out_send, out_recv, extra_send, extra_recv, own,
):
    n, m, rows, block, depth, height, taps = dims
    chans = m * rows
    per = -(-taps // n)
    plane = depth * height
    span = block * plane
    g = lax.axis_index("gx")
    d = lax.axis_index("ch")
    pair, c = lax.div(g, 2), lax.rem(g, 2)

    def level(pp, at):
        return jnp.where(lax.rem(pp, 2) == 0, at, m - 1 - at)

    def device_of(index):
        pp, at = lax.div(index, 2 * m), lax.rem(index, 2 * m)
        return 2 * pp + lax.rem(at, 2), level(pp, lax.div(at, 2))

    place = 2 * level(pair, d) + c
    source, k = lax.div(place, m), lax.rem(place, m)
    holds_own = source == c
    whole = n * m
    spot = pair * 2 * m + place
    prev = device_of(lax.rem(spot + whole - 1, whole))
    following = device_of(lax.rem(spot + 1, whole))

    def worker(q):
        return device_of(pair * 2 * m + c * m + q)

    def holder(dd):
        return 2 * pair + source, dd

    def rows_at(dd):
        return pl.ds(pl.multiple_of(dd * rows, rows), rows)

    def cols_at(kk):
        return pl.ds(pl.multiple_of(kk * span, 128), span)

    barrier = pltpu.get_barrier_semaphore()
    for side in range(2):
        for r in range(m):
            if side + r > 0:
                pl.semaphore_signal(
                    barrier, inc=1, device_id_type=MESH,
                    device_id=(2 * pair + lax.rem(c + side, 2), lax.rem(d + r, m)),
                )
    for r in range(2, n):
        pl.semaphore_signal(
            barrier, inc=1, device_id=(lax.rem(2 * pair + r, n), d), device_id_type=MESH
        )
    pl.semaphore_wait(barrier, 2 * m - 1 + n - 2)

    def remote(src, dst, send, recv, where):
        return pltpu.make_async_remote_copy(
            src_ref=src, dst_ref=dst, send_sem=send, recv_sem=recv,
            device_id=where, device_id_type=MESH,
        )

    mine = pl.ds(g * per, per)

    half = m // 2
    across = lax.rem(d + half, m)
    base = lax.div(d, half) * half

    def w1(sending):
        at = rows_at(d if sending else across)
        return remote(wsl, gathered.at[mine, at, :], w1_send.at[0], w1_recv.at[0], (g, across))

    def w1_share(r, far, sending):
        dd = base + lax.rem(d - base + (r if sending else half - r), half)
        at = d if sending else dd
        part = gathered.at[mine, rows_at(lax.rem(at + half, m) if far else at), :]
        slot = 1 + 2 * (r - 1) + far
        return remote(part, part, w1_send.at[slot], w1_recv.at[slot], (g, dd))

    shares = [(r, far) for r in range(1, half) for far in range(2)]

    def w2(r, sending):
        gg = lax.rem(g + r, n) if sending else lax.rem(g + n - r, n)
        at = g if sending else gg
        part = gathered.at[pl.ds(at * per, per), :, :]
        return remote(part, part, w2_send.at[r], w2_recv.at[r], (gg, d))

    inner = pl.ds(plane, span)

    def spread_out(which, x, field, q):
        return remote(
            field.at[:, cols_at(q)], x.at[rows_at(d), inner],
            in_send.at[which, q], in_recv.at[which, d], worker(q),
        )

    def spread_in(which, x, field, dd):
        return remote(
            field.at[:, cols_at(k)], x.at[rows_at(dd), inner],
            in_send.at[which, k], in_recv.at[which, dd], holder(dd),
        )

    def foreign_work(q):
        return c * m + q != place

    def foreign_holder(dd):
        return jnp.logical_or(jnp.logical_not(holds_own), dd != d)

    low_end, high_end = pl.ds(0, plane), pl.ds(m * span - plane, plane)
    low_slot, high_slot = pl.ds(0, plane), pl.ds(span + plane, plane)
    edges = ((high_end, low_slot, m), (low_end, high_slot, m - 1))

    def extra(which, x, field, side, dd, where):
        src, dst, _ = edges[side]
        return remote(
            field.at[:, src], x.at[rows_at(dd), dst],
            extra_send.at[which], extra_recv.at[which, dd], where,
        )

    def extra_each(which, x, field, act_on):
        for side in range(2):
            @pl.when(jnp.logical_and(c == side, place != edges[side][2]))
            def _():
                act_on(extra(which, x, field, side, d, device_of(pair * 2 * m + edges[side][2])))

    def extra_landed(which, x, field):
        for side in range(2):
            @pl.when(place == edges[side][2])
            def _():
                for r in range(1, m):
                    dd = lax.rem(d + r, m)
                    extra(which, x, field, side, dd, (g, dd)).wait_recv()

    def spread_start(which, x, field, q):
        @pl.when(foreign_work(q))
        def _():
            spread_out(which, x, field, q).start()

    def spread_sent(which, x, field, q):
        @pl.when(foreign_work(q))
        def _():
            spread_out(which, x, field, q).wait_send()

    def spread_landed(which, x, field):
        for dd in range(m):
            @pl.when(foreign_holder(dd))
            def _():
                spread_in(which, x, field, dd).wait_recv()
        extra_landed(which, x, field)

    def spread_own(which, x, field):
        def move(src, dst):
            copy = pltpu.make_async_copy(field.at[:, src], x.at[rows_at(d), dst], own.at[1 + which])
            copy.start()
            copy.wait()

        @pl.when(holds_own)
        def _():
            move(cols_at(k), inner)

        for side in range(2):
            @pl.when(place == edges[side][2])
            def _():
                move(edges[side][0], edges[side][1])

    def halo(which, x, side):
        first, last = pl.ds(plane, plane), pl.ds(span, plane)
        low, high = pl.ds(0, plane), pl.ds(span + plane, plane)
        src, dst, where = ((first, high, prev), (last, low, following))[side]
        return remote(
            x.at[:, src], x.at[:, dst], halo_send.at[which, side], halo_recv.at[which, side], where
        )

    has_prev, has_next = place != m, place != m - 1
    sends, lands = (has_prev, has_next), (has_next, has_prev)

    def halo_start(which, x):
        for side in range(2):
            @pl.when(sends[side])
            def _():
                halo(which, x, side).start()

    def halo_sent(which, x):
        for side in range(2):
            @pl.when(sends[side])
            def _():
                halo(which, x, side).wait_send()

    def halo_landed(which, x):
        for side in range(2):
            @pl.when(lands[side])
            def _():
                halo(which, x, side).wait_recv()

    pieces = [(0, plane), ((block - 1) * plane, plane)]
    if block > 2:
        pieces.append((plane, (block - 2) * plane))

    def collect_out(which, y, out, j, dd):
        at, size = pieces[j]
        return remote(
            y.at[rows_at(dd), pl.ds(at, size)],
            out.at[:, pl.ds(pl.multiple_of(k * span + at, 128), size)],
            out_send.at[which, j, dd], out_recv.at[which, j, k], holder(dd),
        )

    def collect_in(which, y, out, j, q):
        at, size = pieces[j]
        return remote(
            y.at[rows_at(d), pl.ds(at, size)], out.at[:, pl.ds(q * span + at, size)],
            out_send.at[which, j, d], out_recv.at[which, j, q], worker(q),
        )

    def collect_own(which, y, out):
        return pltpu.make_async_copy(y.at[rows_at(d), :], out.at[:, cols_at(k)], own.at[3 + which])

    def collect_start(which, y, out, parts):
        for r in range(m):
            dd = lax.rem(d + r, m)

            @pl.when(foreign_holder(dd))
            def _():
                for j in parts:
                    collect_out(which, y, out, j, dd).start()

    def collect_finish(which, y, out):
        @pl.when(holds_own)
        def _():
            collect_own(which, y, out).wait()

        for q in range(m):
            @pl.when(foreign_work(q))
            def _():
                for j in range(len(pieces)):
                    collect_in(which, y, out, j, q).wait_recv()

            @pl.when(foreign_holder(q))
            def _():
                for j in range(len(pieces)):
                    collect_out(which, y, out, j, q).wait_send()

    for i in range(per):
        wsl[i] = weight[jnp.minimum(g * per + i, taps - 1)]
    peers = range(1, n)
    order = [lax.rem(d + r, m) for r in range(m)]
    w1(True).start()
    for q in order:
        spread_start(0, xa, act, q)
    extra_each(0, xa, act, lambda copy: copy.start())
    for q in order:
        spread_start(1, xg, grad, q)
    extra_each(1, xg, grad, lambda copy: copy.start())
    own_filters = pltpu.make_async_copy(wsl, gathered.at[mine, rows_at(d), :], own.at[0])
    own_filters.start()
    own_filters.wait()
    for r in range(1, half):
        w1_share(r, 0, True).start()
    spread_own(0, xa, act)
    spread_own(1, xg, grad)
    w1(False).wait_recv()
    for r in range(1, half):
        w1_share(r, 1, True).start()
    for r, far in shares:
        w1_share(r, far, False).wait_recv()

    @pl.when(g * per < taps)
    def _():
        for r in peers:
            w2(r, True).start()

    for q in order:
        spread_sent(0, xa, act, q)
    spread_landed(0, xa, act)
    halo_start(0, xa)

    for r in peers:
        @pl.when(lax.rem(g + n - r, n) * per < taps)
        def _():
            w2(r, False).wait_recv()

    def filters(l, backward):
        for a in range(3):
            for b in range(3):
                for e in range(3):
                    tap = 9 * a + 3 * b + e
                    part = gathered[taps - 1 - tap].T if backward else gathered[tap]
                    l[pl.ds(b * chans, chans), pl.ds((3 * e + a) * chans, chans)] = part

    filters(lf, False)
    lane = lax.broadcasted_iota(jnp.int32, (chans, height), 1)

    def pair_sum(x, l, y, pair):
        def cells(slot, z):
            return x[:, pl.ds(slot * plane + z * height, height)]

        for z in range(depth):
            inside = [c for c in range(3) if 0 <= z + c - 1 < depth]
            right = jnp.concatenate(
                [
                    jnp.concatenate([cells(s + a - 1, z + c - 1) for s in pair], axis=1)
                    for c in inside
                    for a in range(3)
                ],
                axis=0,
            )
            left = l[:, pl.ds(inside[0] * 3 * chans, len(inside) * 3 * chans)]
            acc = jnp.dot(left, right, preferred_element_type=jnp.float32)
            for i, s in enumerate(pair):
                part = acc[:, i * height : (i + 1) * height]
                below = pltpu.roll(part[:chans], 1, 1)
                above = pltpu.roll(part[2 * chans :], height - 1, 1)
                total = (
                    part[chans : 2 * chans]
                    + jnp.where(lane > 0, below, 0.0)
                    + jnp.where(lane < height - 1, above, 0.0)
                )
                y[:, pl.ds((s - 1) * plane + z * height, height)] = total.astype(y.dtype)

    def finish(which, x, l, y, out):
        for s in range(2, block, 2):
            pair_sum(x, l, y, (s, s + 1))
        if block > 2:
            collect_start(which, y, out, (2,))
        halo_landed(which, x)
        pair_sum(x, l, y, (1, block))
        collect_start(which, y, out, (0, 1))

        @pl.when(holds_own)
        def _():
            collect_own(which, y, out).start()

    finish(0, xa, lf, yf, outf)
    filters(lb, True)
    spread_landed(1, xg, grad)
    halo_start(1, xg)
    finish(1, xg, lb, yg, outg)

    w1(True).wait_send()
    for r, far in shares:
        w1_share(r, far, True).wait_send()
    for q in order:
        spread_sent(1, xg, grad, q)
    for which, x, field in ((0, xa, act), (1, xg, grad)):
        extra_each(which, x, field, lambda copy: copy.wait_send())
        halo_sent(which, x)
    collect_finish(0, yf, outf)
    collect_finish(1, yg, outg)

    @pl.when(g * per < taps)
    def _():
        for r in peers:
            w2(r, True).wait_send()


def local_kernel(activations, conv_weight, out_grad):
    n, m = lax.axis_size("gx"), lax.axis_size("ch")
    rows, planes, depth, height = activations.shape
    taps, chans, _ = conv_weight.shape
    block = planes // m
    plane = depth * height
    per = -(-taps // n)
    vmem = pl.BlockSpec(memory_space=pltpu.VMEM)
    flat = jax.ShapeDtypeStruct((rows, planes * plane), jnp.bfloat16)
    sem = pltpu.SemaphoreType.DMA
    flops = 2 * 2 * taps * chans * chans * block * plane
    features, gradient = pl.pallas_call(
        functools.partial(kernel, (n, m, rows, block, depth, height, taps)),
        out_shape=(flat, flat),
        in_specs=[vmem] * 3,
        out_specs=(vmem, vmem),
        scratch_shapes=[
            pltpu.VMEM((per, rows, chans), jnp.bfloat16),
            pltpu.VMEM((chans, (block + 2) * plane), jnp.bfloat16),
            pltpu.VMEM((chans, (block + 2) * plane), jnp.bfloat16),
            pltpu.VMEM((per * n, chans, chans), jnp.bfloat16),
            pltpu.VMEM((3 * chans, 9 * chans), jnp.bfloat16),
            pltpu.VMEM((3 * chans, 9 * chans), jnp.bfloat16),
            pltpu.VMEM((chans, block * plane), jnp.bfloat16),
            pltpu.VMEM((chans, block * plane), jnp.bfloat16),
            sem((m,)), sem((m,)), sem((n,)), sem((n,)),
            sem((2, m)), sem((2, m)), sem((2, 2)), sem((2, 2)),
            sem((2, 3, m)), sem((2, 3, m)), sem((2,)), sem((2, m)), sem((5,)),
        ],
        compiler_params=pltpu.CompilerParams(
            collective_id=0, has_side_effects=True, vmem_limit_bytes=20 * 2**20
        ),
        cost_estimate=pl.CostEstimate(
            flops=flops, bytes_accessed=8 * rows * planes * plane, transcendentals=0
        ),
    )(activations.reshape(rows, -1), out_grad.reshape(rows, -1), jnp.swapaxes(conv_weight, 1, 2))
    return features.reshape(activations.shape), gradient.reshape(out_grad.shape)


def local(activations, conv_weight, out_grad):
    n, m = lax.axis_size("gx"), lax.axis_size("ch")
    rows, planes, _, height = activations.shape
    fits = rows % 16 == 0 and planes % (2 * m) == 0 and height % 128 == 0 and n % 4 == 0 and m % 2 == 0
    plan = local_kernel if fits else local_plain
    return plan(activations, conv_weight, out_grad)


def solution(mesh):
    return jax.shard_map(
        local,
        mesh=mesh,
        in_specs=(P("ch", "gx", None, None), P(None, None, "ch"), P("ch", "gx", None, None)),
        out_specs=(P("ch", "gx", None, None), P("ch", "gx", None, None)),
        check_vma=False,
    )
```
